32 devices in a mesh: tm: 4 (over y, core), chan: 8 (over z, x).
Axes of the slice: x: 2, y: 2, z: 4, core: 2. Of those that a mesh axis runs over, the one named last changes fastest.
Arguments:
- filterbank: bfloat16 [1024, 1024], P('chan', 'tm'), may hold values from -6 to 6
- chan_delay: int32 [1024], replicated, may hold values from 0 to 4096, as said below
- tail_len: int32 [32], replicated, may hold values from 1 to 256, as said below
- kernels: bfloat16 [2, 32, 256], replicated, may hold values from -0.375 to 0.375
Outputs:
- accel_power: bfloat16 [32, 32, 512], P(None, 'chan', 'tm')
The draws below stay inside these ranges and needn't reach their ends.
Inputs may be any that keep to these rules, and one draw needn't show every extreme that they name: `chan_delay`: some channel has exactly 4096. `tail_len`: some trial has exactly 256.
All inputs are finite; a program needn't handle non-finite values.
Results may differ from the reference program's by a relative error of at most 0.011.
Values may be sent and summed in bfloat16 or wider, within the bound.
No kernel may reach another device: no remote copies, remote signals or barrier semaphores. Data moves between devices by JAX's collectives and lax.ppermute only.
A program may use at most 64 MiB of HBM per device.

```python
import math
import jax
import jax.numpy as jnp
from jax import lax

CHANNELS = 1024
TRIAL_DEV = 4
BLOCK = 256
MAXDELAY = 4096
ACCELS = 32
TAPS = 256
TRIALS = 32
SAMPLES = 1024
N_TM = 4


def draw_chan_delay(key, part):
    value_key = jax.random.fold_in(key, 11)
    chosen_key = jax.random.fold_in(key, 12)
    values = jax.random.randint(value_key, (CHANNELS,), 0, MAXDELAY + 1, dtype=jnp.int32)
    chosen = jax.random.randint(chosen_key, (), 0, CHANNELS, dtype=jnp.int32)
    return jnp.where(jnp.arange(CHANNELS, dtype=jnp.int32) == chosen, MAXDELAY, values).astype(jnp.int32)


def draw_tail_len(key, part):
    value_key = jax.random.fold_in(key, 21)
    chosen_key = jax.random.fold_in(key, 22)
    values = jax.random.randint(value_key, (TRIALS,), 1, BLOCK + 1, dtype=jnp.int32)
    chosen = jax.random.randint(chosen_key, (), 0, TRIALS, dtype=jnp.int32)
    return jnp.where(jnp.arange(TRIALS, dtype=jnp.int32) == chosen, BLOCK, values).astype(jnp.int32)


def block_scale(stream_key, shape, shards, smallest, top_value):
    loudness = 1.0
    for dim, shards_of in shards:
        heights = jax.random.uniform(jax.random.fold_in(jax.random.fold_in(stream_key, 6), dim), (shards_of,), jnp.float32, smallest / len(shards), top_value / len(shards))
        loudness = loudness * jnp.repeat(jnp.exp(heights), shape[dim] // shards_of).reshape((-1,) + (1,) * (len(shape) - 1 - dim))
    return loudness


def gaussian(rng, dims, width, bound, cuts=(), held_as=jnp.bfloat16):
    array = width * jax.random.normal(rng, dims, jnp.float32)
    if cuts:
        array = array * block_scale(rng, dims, cuts, -0.22, 0.18)
    return jnp.clip(array, -bound, bound).astype(held_as)


def setup_inputs(seed: int = 0) -> dict:
    splits = jax.random.split(jax.random.key(seed), 5)
    return {
        "filterbank": gaussian(splits[0], (CHANNELS, SAMPLES), 1.0, 6.0, ((0, 8), (1, 4))),
        "chan_delay": draw_chan_delay(jax.random.fold_in(splits[4], 71), 0),
        "tail_len": draw_tail_len(jax.random.fold_in(splits[4], 71), 0),
        "kernels": gaussian(splits[3], (2, ACCELS, TAPS), TAPS ** -0.5, 0.375),
    }


def forward_table(block_len):
    period = 2 * block_len
    sample_idx = jnp.arange(block_len, dtype=jnp.int32)
    phases = sample_idx[:, None] * sample_idx[None, :] % period
    angles = phases.astype(jnp.float32) * (2.0 * math.pi / period)
    return jnp.concatenate([jnp.cos(angles), -jnp.sin(angles)], axis=1).astype(jnp.bfloat16)

def inverse_table(block_len):
    period = 2 * block_len
    bin_index = jnp.arange(block_len, dtype=jnp.int32)
    position = jnp.arange(period, dtype=jnp.int32)
    offsets = (position + block_len) % period
    phases = bin_index[:, None] * offsets[None, :] % period
    angles = phases.astype(jnp.float32) * (2.0 * math.pi / period)
    weights = jnp.where(bin_index == 0, 1.0, 2.0).astype(jnp.bfloat16)[:, None]
    cosines = jnp.cos(angles).astype(jnp.bfloat16)
    sine_vals = jnp.sin(angles).astype(jnp.bfloat16)
    return jnp.concatenate([cosines * weights, -(sine_vals * weights)], axis=0)

def block_table(block_len):
    half_len = block_len // 2
    sample_idx = jnp.arange(block_len, dtype=jnp.int32)
    bin_index = jnp.arange(half_len, dtype=jnp.int32)
    phases = sample_idx[:, None] * bin_index[None, :] % block_len
    angles = phases.astype(jnp.float32) * (2.0 * math.pi / block_len)
    return jnp.concatenate([jnp.cos(angles), -jnp.sin(angles)], axis=1).astype(jnp.bfloat16)

def kernel_weights(kernels):
    real_kernel = kernels[0]
    imag_kernel = kernels[1]
    upper_rows = jnp.stack([real_kernel, -imag_kernel], axis=1)
    lower_rows = jnp.stack([imag_kernel, real_kernel], axis=1)
    return jnp.concatenate([upper_rows, lower_rows], axis=0)

def correlate(block_spectra, weights, tap_count):
    return lax.conv_general_dilated(block_spectra, weights, (1,), [(tap_count // 2, tap_count - 1 - tap_count // 2)], preferred_element_type=jnp.float32)

def reference(filterbank, chan_delay, tail_len, kernels):
    block_len = BLOCK
    period = 2 * block_len
    half_len = block_len // 2
    forward = forward_table(block_len)
    inverse = inverse_table(block_len)
    blocked = block_table(block_len)
    shifts = chan_delay[:, None] * tail_len[None, :] // MAXDELAY
    lookup = jnp.arange(period, dtype=jnp.int32).astype(jnp.float32) * (2.0 * math.pi / period)
    cos_lookup = jnp.cos(lookup).astype(jnp.bfloat16).astype(jnp.float32)
    sin_lookup = jnp.sin(lookup).astype(jnp.bfloat16).astype(jnp.float32)
    bin_index = jnp.arange(block_len, dtype=jnp.int32)
    trial_blocks = TRIALS // TRIAL_DEV

    def one_group(group_index):
        samples = lax.dynamic_slice_in_dim(filterbank, group_index * block_len, block_len, axis=1)
        spectra = (jnp.dot(samples, forward, preferred_element_type=jnp.float32) * (1.0 / math.sqrt(block_len))).astype(jnp.bfloat16)
        real_part = spectra[:, :block_len].astype(jnp.float32)
        imag_part = spectra[:, block_len:].astype(jnp.float32)

        def trial_block(first_trial):
            part_shifts = lax.dynamic_slice_in_dim(shifts, first_trial, TRIAL_DEV, axis=1)
            phases = part_shifts[:, :, None] * bin_index[None, None, :] % period
            ramp_cos = jnp.take(cos_lookup, phases)
            ramp_sin = jnp.take(sin_lookup, phases)
            out_real = jnp.einsum('ck,cdk->dk', real_part, ramp_cos) - jnp.einsum('ck,cdk->dk', imag_part, ramp_sin)
            out_imag = jnp.einsum('ck,cdk->dk', real_part, ramp_sin) + jnp.einsum('ck,cdk->dk', imag_part, ramp_cos)
            return jnp.concatenate([out_real, out_imag], axis=1) * (1.0 / math.sqrt(CHANNELS))
        firsts = jnp.arange(trial_blocks, dtype=jnp.int32) * TRIAL_DEV
        dedispersed = lax.map(trial_block, firsts).reshape(TRIALS, 2 * block_len)
        return jnp.dot(dedispersed.astype(jnp.bfloat16), inverse, preferred_element_type=jnp.float32) * (0.5 / math.sqrt(block_len))
    block_series = lax.map(one_group, jnp.arange(N_TM, dtype=jnp.int32))
    positions = jnp.arange(block_len, dtype=jnp.int32)
    keep_mask = positions[None, :] >= block_len - tail_len[:, None]
    tail_parts = jnp.where(keep_mask[None], block_series[:, :, :block_len], 0.0)
    following = jnp.concatenate([tail_parts[1:], jnp.zeros_like(tail_parts[:1])], axis=0)
    series = (block_series[:, :, block_len:] + following).astype(jnp.bfloat16)
    spectra_blocks = (jnp.dot(series.reshape(N_TM * TRIALS, block_len), blocked, preferred_element_type=jnp.float32) * (1.0 / math.sqrt(block_len))).astype(jnp.bfloat16)
    spectra_blocks = spectra_blocks.reshape(N_TM * TRIALS, 2, half_len).astype(jnp.float32)
    weights = kernel_weights(kernels.astype(jnp.float32))
    correlation = correlate(spectra_blocks, weights, TAPS)
    power_out = correlation[:, :ACCELS] * correlation[:, :ACCELS] + correlation[:, ACCELS:] * correlation[:, ACCELS:]
    power_out = power_out.reshape(N_TM, TRIALS, ACCELS, half_len).transpose(2, 1, 0, 3).reshape(ACCELS, TRIALS, N_TM * half_len)
    return power_out.astype(jnp.bfloat16)
```

```python
import functools
import math

import jax
import jax.numpy as jnp
import numpy as np
from jax import lax
from jax.experimental import pallas as pl
from jax.experimental.pallas import tpu as pltpu
from jax.sharding import PartitionSpec as P

TRIAL_DEV = 4
MAXDELAY = 4096
LANES = 128
FINE = 16
COARSE = LANES // FINE
ROWS = 2 * TRIAL_DEV


def bin_table(block_len):
    half_len = block_len // 2
    samples = np.arange(half_len)
    angles = (samples[:, None] * samples[None, :] % block_len) * (2.0 * math.pi / block_len)
    table = np.concatenate([np.cos(angles), -np.sin(angles)], axis=1)
    return jnp.asarray(table.astype(np.float32), jnp.bfloat16)


def shift_left(value, steps):
    width = value.shape[1]
    return pltpu.roll(value, width - steps, 1)


def as_column(row):
    count = row.shape[1]
    rows = lax.broadcasted_iota(jnp.int32, (count, count), 0)
    columns = lax.broadcasted_iota(jnp.int32, (count, count), 1)
    return jnp.sum(jnp.where(rows == columns, row, 0), axis=1, keepdims=True)


def trial_blocks(value, chan_count):
    parts = []
    for owner in range(chan_count):
        rows = value[owner * TRIAL_DEV : (owner + 1) * TRIAL_DEV]
        parts += [rows[:, :LANES], rows[:, LANES:]]
    return jnp.concatenate(parts, axis=0).astype(jnp.bfloat16)


def partial_series(tm_count, chan_count, samples_ref, delay_ref, tail_ref, out_ref, moved, chosen):
    channels, block_len = samples_ref.shape
    trials = tail_ref.shape[1]
    samples = samples_ref[...]
    padded = jnp.concatenate([jnp.zeros((channels, LANES), jnp.bfloat16), samples], axis=1)
    for coarse in range(COARSE):
        moved[coarse * channels : (coarse + 1) * channels, :] = (
            shift_left(padded, FINE * coarse) if coarse else padded
        )

    delays = delay_ref[pl.ds(lax.axis_index("chan"), 1), :]
    tails = as_column(tail_ref[...])
    shifts = lax.shift_right_logical(delays * tails, MAXDELAY.bit_length() - 1)
    shift_vals = shifts.astype(jnp.float32)
    rests = jnp.concatenate([shift_vals - FINE * coarse for coarse in range(COARSE)], axis=1)
    rests = rests.astype(jnp.bfloat16)
    one = jnp.ones((), jnp.bfloat16)
    zero = jnp.zeros((), jnp.bfloat16)
    for part in range(2):
        for fine in range(FINE):
            first = (part * FINE + fine) * trials
            wanted = jnp.array(part * LANES + fine, jnp.bfloat16)
            chosen[first : first + trials, :] = jnp.where(rests == wanted, one, zero)
    sums = jnp.dot(chosen[...], moved[...], preferred_element_type=jnp.float32)

    level = []
    for fine in range(FINE):
        near = sums[fine * trials : (fine + 1) * trials]
        far = sums[(FINE + fine) * trials : (FINE + fine + 1) * trials]
        level.append(
            jnp.concatenate(
                [
                    far[:, :LANES],
                    far[:, LANES : 2 * LANES] + near[:, :LANES],
                    far[:, 2 * LANES :] + near[:, LANES : 2 * LANES],
                    near[:, 2 * LANES :],
                ],
                axis=1,
            )
        )
    steps = 1
    while len(level) > 1:
        level = [
            level[2 * i] + shift_left(level[2 * i + 1], steps) for i in range(len(level) // 2)
        ]
        steps *= 2
    series = level[0]

    rows = lax.broadcasted_iota(jnp.int32, (block_len, LANES), 0)
    columns = lax.broadcasted_iota(jnp.int32, (block_len, LANES), 1)
    nyquist_step = 0.5 / block_len
    alternating = jnp.where((rows + columns) % 2 == 0, -nyquist_step, nyquist_step)
    nyquist = jnp.dot(samples, alternating.astype(jnp.bfloat16), preferred_element_type=jnp.float32)
    parity = jnp.where(shifts % 2 == 0, 1.0, -1.0).astype(jnp.bfloat16)
    top_bin = jnp.dot(parity, nyquist.astype(jnp.bfloat16), preferred_element_type=jnp.float32)
    top_bin = jnp.concatenate([top_bin, top_bin], axis=1)
    whole = jnp.where(shifts == block_len, 1.0, 0.0).astype(jnp.bfloat16)
    whole_block = jnp.dot(whole, samples, preferred_element_type=jnp.float32)

    scale = 1.0 / math.sqrt(channels * chan_count)
    late = (series[:, block_len:] + top_bin) * scale
    early = (series[:, :block_len] + top_bin + whole_block) * scale
    positions = lax.broadcasted_iota(jnp.int32, (trials, block_len), 1)
    early = jnp.where(positions >= block_len - tails, early, 0.0)

    group_rows = chan_count * ROWS
    group = lax.axis_index("tm")
    out_ref[...] = jnp.zeros_like(out_ref)
    out_ref[pl.ds(pl.multiple_of(group * group_rows, group_rows), group_rows), :] = trial_blocks(
        late, chan_count
    )

    @pl.when(group > 0)
    def _():
        before = pl.multiple_of((group - 1) * group_rows, group_rows)
        out_ref[pl.ds(before, group_rows), :] = trial_blocks(early, chan_count)


def accel_search(tm_count, chan_count, parts_ref, table_ref, kernels_ref, out_ref):
    group_rows = chan_count * ROWS
    group = lax.axis_index("tm")
    after = lax.rem(group + 1, tm_count)
    own = parts_ref[pl.ds(pl.multiple_of(group * group_rows, group_rows), group_rows), :]
    following = parts_ref[pl.ds(pl.multiple_of(after * group_rows, group_rows), group_rows), :]
    both = own.astype(jnp.float32) + following.astype(jnp.float32)
    series = jnp.sum(both.reshape(chan_count, ROWS, LANES), axis=0).astype(jnp.bfloat16)

    half_len = LANES
    block_len = 2 * half_len
    halves = jnp.dot(series, table_ref[...], preferred_element_type=jnp.float32)
    columns = lax.broadcasted_iota(jnp.int32, (TRIAL_DEV, block_len), 1)
    signs = jnp.where(columns % 2 == 0, 1.0, -1.0)
    spectra = (halves[:TRIAL_DEV] + signs * halves[TRIAL_DEV:]) * (1.0 / math.sqrt(block_len))
    spectra = spectra.astype(jnp.bfloat16).astype(jnp.float32)

    sublanes = lax.broadcasted_iota(jnp.int32, (8, block_len), 0)
    zeros = jnp.zeros((8, half_len), jnp.float32)
    taps = []
    for trial in range(TRIAL_DEV):
        windows = []
        for first in (0, half_len):
            row = spectra[trial : trial + 1, first : first + half_len]
            wide = jnp.concatenate([zeros, jnp.broadcast_to(row, (8, half_len))], axis=1)
            for steps in (1, 2, 4):
                wide = jnp.where(sublanes & steps != 0, shift_left(wide, steps), wide)
            for start in range(0, block_len, 8):
                windows.append((shift_left(wide, start) if start else wide)[:, :half_len])
        taps.append(jnp.concatenate(windows, axis=0).astype(jnp.bfloat16))
    windows = jnp.concatenate(taps, axis=1)

    real = kernels_ref[0]
    imag = kernels_ref[1]
    weights = jnp.concatenate(
        [jnp.concatenate([real, -imag], axis=1), jnp.concatenate([imag, real], axis=1)], axis=0
    )
    correlation = jnp.dot(weights, windows, preferred_element_type=jnp.float32)
    accels = real.shape[0]
    power = correlation[:accels] * correlation[:accels] + correlation[accels:] * correlation[accels:]
    for trial in range(TRIAL_DEV):
        out_ref[:, trial, :] = power[:, trial * half_len : (trial + 1) * half_len].astype(
            jnp.bfloat16
        )


def shards(tm_count, chan_count, filterbank, chan_delay, tail_len, kernels):
    channels, block_len = filterbank.shape
    trials = tail_len.shape[0]
    accels = kernels.shape[1]
    devices = tm_count * chan_count
    parts = pl.pallas_call(
        functools.partial(partial_series, tm_count, chan_count),
        out_shape=jax.ShapeDtypeStruct((devices * ROWS, LANES), jnp.bfloat16),
        scratch_shapes=[
            pltpu.VMEM((COARSE * channels, block_len + LANES), jnp.bfloat16),
            pltpu.VMEM((2 * FINE * trials, COARSE * channels), jnp.bfloat16),
        ],
        compiler_params=pltpu.CompilerParams(vmem_limit_bytes=40 * 1024 * 1024),
        name="partial_series",
    )(filterbank, chan_delay.reshape(chan_count, channels), tail_len.reshape(1, trials))
    parts = lax.all_to_all(parts, ("tm", "chan"), 0, 0, tiled=True)
    return pl.pallas_call(
        functools.partial(accel_search, tm_count, chan_count),
        out_shape=jax.ShapeDtypeStruct((accels, TRIAL_DEV, block_len // 2), jnp.bfloat16),
        compiler_params=pltpu.CompilerParams(vmem_limit_bytes=40 * 1024 * 1024),
        name="accel_search",
    )(parts, bin_table(block_len), kernels)


def solution(mesh):
    placed = (P("chan", "tm"), P(), P(), P())
    return jax.shard_map(
        functools.partial(shards, mesh.shape["tm"], mesh.shape["chan"]),
        mesh=mesh,
        in_specs=placed,
        out_specs=P(None, "chan", "tm"),
        check_vma=False,
    )
```

```python
import functools
import math

import jax
import jax.numpy as jnp
import numpy as np
from jax import lax
from jax.experimental import pallas as pl
from jax.experimental.pallas import tpu as pltpu
from jax.sharding import PartitionSpec as P

TRIAL_DEV = 4
MAXDELAY = 4096
LANES = 128
FINE = 16
COARSE = LANES // FINE
ROWS = 2 * TRIAL_DEV


def bin_table(block_len):
    half_len = block_len // 2
    samples = np.arange(half_len)
    angles = (samples[:, None] * samples[None, :] % block_len) * (2.0 * math.pi / block_len)
    table = np.concatenate([np.cos(angles), -np.sin(angles)], axis=1)
    return jnp.asarray(table.astype(np.float32), jnp.bfloat16)


def shift_left(value, steps):
    width = value.shape[1]
    return pltpu.roll(value, width - steps, 1)


def as_column(row):
    count = row.shape[1]
    rows = lax.broadcasted_iota(jnp.int32, (count, count), 0)
    columns = lax.broadcasted_iota(jnp.int32, (count, count), 1)
    return jnp.sum(jnp.where(rows == columns, row, 0), axis=1, keepdims=True)


def trial_blocks(value, chan_count):
    parts = []
    for owner in range(chan_count):
        rows = value[owner * TRIAL_DEV : (owner + 1) * TRIAL_DEV]
        parts += [rows[:, :LANES], rows[:, LANES:]]
    return jnp.concatenate(parts, axis=0).astype(jnp.bfloat16)


def partial_series(
    tm_count,
    chan_count,
    samples_hbm,
    delay_hbm,
    tail_hbm,
    out_ref,
    samples_ref,
    delay_ref,
    tail_ref,
    moved,
    chosen,
    arrived,
):
    channels, block_len = samples_ref.shape
    trials = tail_ref.shape[1]
    copies = [
        pltpu.make_async_copy(source, target, arrived.at[index])
        for index, (source, target) in enumerate(
            [(delay_hbm, delay_ref), (tail_hbm, tail_ref), (samples_hbm, samples_ref)]
        )
    ]
    for copy in copies:
        copy.start()
    out_ref[...] = jnp.zeros_like(out_ref)
    for copy in copies:
        copy.wait()
    samples = samples_ref[...]
    padded = jnp.concatenate([jnp.zeros((channels, LANES), jnp.bfloat16), samples], axis=1)
    for coarse in range(COARSE):
        moved[coarse * channels : (coarse + 1) * channels, :] = (
            shift_left(padded, FINE * coarse) if coarse else padded
        )

    delays = delay_ref[pl.ds(lax.axis_index("chan"), 1), :]
    tails = as_column(tail_ref[...])
    shifts = lax.shift_right_logical(delays * tails, MAXDELAY.bit_length() - 1)
    shift_vals = shifts.astype(jnp.float32)
    rests = jnp.concatenate([shift_vals - FINE * coarse for coarse in range(COARSE)], axis=1)
    rests = rests.astype(jnp.bfloat16)
    one = jnp.ones((), jnp.bfloat16)
    zero = jnp.zeros((), jnp.bfloat16)
    for part in range(2):
        for fine in range(FINE):
            first = (part * FINE + fine) * trials
            wanted = jnp.array(part * LANES + fine, jnp.bfloat16)
            chosen[first : first + trials, :] = jnp.where(rests == wanted, one, zero)
    sums = jnp.dot(chosen[...], moved[...], preferred_element_type=jnp.float32)

    level = []
    for fine in range(FINE):
        near = sums[fine * trials : (fine + 1) * trials]
        far = sums[(FINE + fine) * trials : (FINE + fine + 1) * trials]
        level.append(
            jnp.concatenate(
                [
                    far[:, :LANES],
                    far[:, LANES : 2 * LANES] + near[:, :LANES],
                    far[:, 2 * LANES :] + near[:, LANES : 2 * LANES],
                    near[:, 2 * LANES :],
                ],
                axis=1,
            )
        )
    steps = 1
    while len(level) > 1:
        level = [
            level[2 * i] + shift_left(level[2 * i + 1], steps) for i in range(len(level) // 2)
        ]
        steps *= 2
    series = level[0]

    rows = lax.broadcasted_iota(jnp.int32, (block_len, LANES), 0)
    columns = lax.broadcasted_iota(jnp.int32, (block_len, LANES), 1)
    nyquist_step = 0.5 / block_len
    alternating = jnp.where((rows + columns) % 2 == 0, -nyquist_step, nyquist_step)
    nyquist = jnp.dot(samples, alternating.astype(jnp.bfloat16), preferred_element_type=jnp.float32)
    parity = jnp.where(shifts % 2 == 0, 1.0, -1.0).astype(jnp.bfloat16)
    top_bin = jnp.dot(parity, nyquist.astype(jnp.bfloat16), preferred_element_type=jnp.float32)
    top_bin = jnp.concatenate([top_bin, top_bin], axis=1)
    whole = jnp.where(shifts == block_len, 1.0, 0.0).astype(jnp.bfloat16)
    whole_block = jnp.dot(whole, samples, preferred_element_type=jnp.float32)

    scale = 1.0 / math.sqrt(channels * chan_count)
    late = (series[:, block_len:] + top_bin) * scale
    early = (series[:, :block_len] + top_bin + whole_block) * scale
    positions = lax.broadcasted_iota(jnp.int32, (trials, block_len), 1)
    early = jnp.where(positions >= block_len - tails, early, 0.0)

    group_rows = chan_count * ROWS
    group = lax.axis_index("tm")
    out_ref[pl.ds(pl.multiple_of(group * group_rows, group_rows), group_rows), :] = trial_blocks(
        late, chan_count
    )

    @pl.when(group > 0)
    def _():
        before = pl.multiple_of((group - 1) * group_rows, group_rows)
        out_ref[pl.ds(before, group_rows), :] = trial_blocks(early, chan_count)


def accel_search(tm_count, chan_count, parts_ref, table_ref, kernels_ref, out_ref):
    group_rows = chan_count * ROWS
    group = lax.axis_index("tm")
    after = lax.rem(group + 1, tm_count)
    own = parts_ref[pl.ds(pl.multiple_of(group * group_rows, group_rows), group_rows), :]
    following = parts_ref[pl.ds(pl.multiple_of(after * group_rows, group_rows), group_rows), :]
    both = own.astype(jnp.float32) + following.astype(jnp.float32)
    series = jnp.sum(both.reshape(chan_count, ROWS, LANES), axis=0).astype(jnp.bfloat16)

    half_len = LANES
    block_len = 2 * half_len
    halves = jnp.dot(series, table_ref[...], preferred_element_type=jnp.float32)
    columns = lax.broadcasted_iota(jnp.int32, (TRIAL_DEV, block_len), 1)
    signs = jnp.where(columns % 2 == 0, 1.0, -1.0)
    spectra = (halves[:TRIAL_DEV] + signs * halves[TRIAL_DEV:]) * (1.0 / math.sqrt(block_len))
    spectra = spectra.astype(jnp.bfloat16).astype(jnp.float32)

    sublanes = lax.broadcasted_iota(jnp.int32, (8, block_len), 0)
    zeros = jnp.zeros((8, half_len), jnp.float32)
    taps = []
    for trial in range(TRIAL_DEV):
        windows = []
        for first in (0, half_len):
            row = spectra[trial : trial + 1, first : first + half_len]
            wide = jnp.concatenate([zeros, jnp.broadcast_to(row, (8, half_len))], axis=1)
            for steps in (1, 2, 4):
                wide = jnp.where(sublanes & steps != 0, shift_left(wide, steps), wide)
            for start in range(0, block_len, 8):
                windows.append((shift_left(wide, start) if start else wide)[:, :half_len])
        taps.append(jnp.concatenate(windows, axis=0).astype(jnp.bfloat16))
    windows = jnp.concatenate(taps, axis=1)

    real = kernels_ref[0]
    imag = kernels_ref[1]
    weights = jnp.concatenate(
        [jnp.concatenate([real, -imag], axis=1), jnp.concatenate([imag, real], axis=1)], axis=0
    )
    correlation = jnp.dot(weights, windows, preferred_element_type=jnp.float32)
    accels = real.shape[0]
    power = correlation[:accels] * correlation[:accels] + correlation[accels:] * correlation[accels:]
    for trial in range(TRIAL_DEV):
        out_ref[:, trial, :] = power[:, trial * half_len : (trial + 1) * half_len].astype(
            jnp.bfloat16
        )


def shards(tm_count, chan_count, filterbank, chan_delay, tail_len, kernels):
    channels, block_len = filterbank.shape
    trials = tail_len.shape[0]
    accels = kernels.shape[1]
    devices = tm_count * chan_count
    parts = pl.pallas_call(
        functools.partial(partial_series, tm_count, chan_count),
        out_shape=jax.ShapeDtypeStruct((devices * ROWS, LANES), jnp.bfloat16),
        in_specs=[pl.BlockSpec(memory_space=pltpu.HBM)] * 3,
        scratch_shapes=[
            pltpu.VMEM((channels, block_len), jnp.bfloat16),
            pltpu.VMEM((chan_count, channels), jnp.int32),
            pltpu.VMEM((1, trials), jnp.int32),
            pltpu.VMEM((COARSE * channels, block_len + LANES), jnp.bfloat16),
            pltpu.VMEM((2 * FINE * trials, COARSE * channels), jnp.bfloat16),
            pltpu.SemaphoreType.DMA((3,)),
        ],
        compiler_params=pltpu.CompilerParams(vmem_limit_bytes=40 * 1024 * 1024),
        name="partial_series",
    )(
        *(
            pltpu.with_memory_space_constraint(value, pltpu.HBM)
            for value in (
                filterbank,
                chan_delay.reshape(chan_count, channels),
                tail_len.reshape(1, trials),
            )
        )
    )
    parts = lax.all_to_all(parts, ("tm", "chan"), 0, 0, tiled=True)
    return pl.pallas_call(
        functools.partial(accel_search, tm_count, chan_count),
        out_shape=jax.ShapeDtypeStruct((accels, TRIAL_DEV, block_len // 2), jnp.bfloat16),
        compiler_params=pltpu.CompilerParams(vmem_limit_bytes=40 * 1024 * 1024),
        name="accel_search",
    )(parts, bin_table(block_len), kernels)


def solution(mesh):
    placed = (P("chan", "tm"), P(), P(), P())
    return jax.shard_map(
        functools.partial(shards, mesh.shape["tm"], mesh.shape["chan"]),
        mesh=mesh,
        in_specs=placed,
        out_specs=P(None, "chan", "tm"),
        check_vma=False,
    )
```

```python
import functools
import math

import jax
import jax.numpy as jnp
import numpy as np
from jax import lax
from jax.experimental import pallas as pl
from jax.experimental.pallas import tpu as pltpu
from jax.sharding import PartitionSpec as P

TRIAL_DEV = 4
MAXDELAY = 4096
LANES = 128
STEP = 8
ROWS = 2 * TRIAL_DEV


def bin_table(block_len):
    half_len = block_len // 2
    samples = np.arange(half_len)
    angles = (samples[:, None] * samples[None, :] % block_len) * (2.0 * math.pi / block_len)
    table = np.concatenate([np.cos(angles), -np.sin(angles)], axis=1)
    return jnp.asarray(table.astype(np.float32), jnp.bfloat16)


def shift_left(value, steps):
    width = value.shape[1]
    return pltpu.roll(value, width - steps, 1)


def as_column(row):
    count = row.shape[1]
    rows = lax.broadcasted_iota(jnp.int32, (count, count), 0)
    columns = lax.broadcasted_iota(jnp.int32, (count, count), 1)
    return jnp.sum(jnp.where(rows == columns, row, 0.0), axis=1, keepdims=True)


def trial_blocks(value, chan_count):
    parts = []
    for owner in range(chan_count):
        rows = value[owner * TRIAL_DEV : (owner + 1) * TRIAL_DEV]
        parts += [rows[:, :LANES], rows[:, LANES:]]
    return jnp.concatenate(parts, axis=0).astype(jnp.bfloat16)


def partial_series(
    tm_count,
    chan_count,
    samples_hbm,
    delay_hbm,
    tail_hbm,
    out_ref,
    samples_ref,
    delay_ref,
    tail_ref,
    turned,
    moved,
    chosen,
    total,
    arrived,
):
    channels, block_len = samples_ref.shape
    trials = tail_ref.shape[1]
    repeats = max(1, LANES // trials)
    width = repeats * trials
    groups = block_len // (STEP * repeats)
    pair = max(1, 2 * LANES // width)
    copies = [
        pltpu.make_async_copy(source, target, arrived.at[index])
        for index, (source, target) in enumerate(
            [(delay_hbm, delay_ref), (tail_hbm, tail_ref), (samples_hbm, samples_ref)]
        )
    ]
    for copy in copies:
        copy.start()
    out_ref[...] = jnp.zeros_like(out_ref)
    copies[0].wait()
    copies[1].wait()

    delays = as_column(delay_ref[pl.ds(lax.axis_index("chan"), 1), :].astype(jnp.float32))
    tails = jnp.concatenate([tail_ref[...].astype(jnp.float32)] * repeats, axis=1)
    shifts = jnp.floor(delays * tails * (1.0 / MAXDELAY))
    columns = lax.broadcasted_iota(jnp.int32, (channels, width), 1)
    rests = (shifts - STEP * (columns // trials).astype(jnp.float32)).astype(jnp.bfloat16)
    one = jnp.ones((), jnp.bfloat16)
    zero = jnp.zeros((), jnp.bfloat16)

    def where_rest_is(value):
        return jnp.where(rests == jnp.array(value, jnp.bfloat16), one, zero)

    def choose(first):
        for fine in range(STEP):
            for group in range(first, min(first + pair, groups)):
                chosen[
                    fine * channels : (fine + 1) * channels, group * width : (group + 1) * width
                ] = where_rest_is(STEP * repeats * group + fine)

    choose(0)
    whole = where_rest_is(block_len)
    parity = jnp.where(shifts - 2.0 * jnp.floor(shifts * 0.5) == 0.0, one, -one)

    copies[2].wait()
    rows = moved.shape[0]
    turned[:STEP] = jnp.zeros((STEP, channels), jnp.float32)
    turned[STEP : STEP + block_len] = samples_ref[...].astype(jnp.float32).T
    turned[STEP + block_len :] = jnp.zeros((2 * STEP, channels), jnp.float32)
    for fine in range(STEP):
        moved[:, fine * channels : (fine + 1) * channels] = turned[fine : fine + rows].astype(
            jnp.bfloat16
        )
    unmoved = moved[:, :channels]
    whole_sums = jnp.dot(unmoved, whole, preferred_element_type=jnp.float32)
    signs = lax.broadcasted_iota(jnp.int32, (STEP, rows), 0)
    signs += lax.broadcasted_iota(jnp.int32, (STEP, rows), 1)
    nyquist_step = 0.5 / block_len
    alternating = jnp.where(signs % 2 == 0, -nyquist_step, nyquist_step).astype(jnp.bfloat16)
    nyquist = jnp.dot(alternating, unmoved, preferred_element_type=jnp.float32)
    top_bin = jnp.dot(nyquist.astype(jnp.bfloat16), parity, preferred_element_type=jnp.float32)
    top_bin = jnp.where(columns[:STEP] < trials, top_bin, 0.0)

    sublanes = lax.broadcasted_iota(jnp.int32, (STEP, width), 0)
    chunks = block_len // STEP
    for chunk in range(2 * chunks):
        start = top_bin
        if chunk < chunks:
            positions = (sublanes + chunk * STEP).astype(jnp.float32)
            start = jnp.where(positions >= block_len - tails, top_bin, 0.0)
            start += whole_sums[(chunk + 1) * STEP : (chunk + 2) * STEP]
        total[chunk * STEP : (chunk + 1) * STEP] = start
    for first in range(0, groups, pair):
        if first + pair < groups:
            choose(first + pair)
        last = min(first + pair, groups)
        sums = jnp.dot(
            moved[...], chosen[:, first * width : last * width], preferred_element_type=jnp.float32
        )
        for group in range(first, last):
            start = block_len - STEP - STEP * repeats * group
            columns_of = slice((group - first) * width, (group - first + 1) * width)
            total[start : start + block_len + STEP] += sums[: block_len + STEP, columns_of]
    turned_back = total[...].T
    series = turned_back[:trials]
    for repeat in range(1, repeats):
        series += shift_left(turned_back[repeat * trials : (repeat + 1) * trials], repeat * STEP)
    series *= 1.0 / math.sqrt(channels * chan_count)

    group_rows = chan_count * ROWS
    group = lax.axis_index("tm")
    out_ref[pl.ds(pl.multiple_of(group * group_rows, group_rows), group_rows), :] = trial_blocks(
        series[:, block_len:], chan_count
    )

    @pl.when(group > 0)
    def _():
        before = pl.multiple_of((group - 1) * group_rows, group_rows)
        out_ref[pl.ds(before, group_rows), :] = trial_blocks(series[:, :block_len], chan_count)


def accel_search(tm_count, chan_count, parts_ref, table_ref, kernels_ref, out_ref):
    group_rows = chan_count * ROWS
    group = lax.axis_index("tm")
    after = lax.rem(group + 1, tm_count)
    own = parts_ref[pl.ds(pl.multiple_of(group * group_rows, group_rows), group_rows), :]
    following = parts_ref[pl.ds(pl.multiple_of(after * group_rows, group_rows), group_rows), :]
    both = own.astype(jnp.float32) + following.astype(jnp.float32)
    series = jnp.sum(both.reshape(chan_count, ROWS, LANES), axis=0).astype(jnp.bfloat16)

    half_len = LANES
    block_len = 2 * half_len
    halves = jnp.dot(series, table_ref[...], preferred_element_type=jnp.float32)
    columns = lax.broadcasted_iota(jnp.int32, (TRIAL_DEV, block_len), 1)
    signs = jnp.where(columns % 2 == 0, 1.0, -1.0)
    spectra = (halves[:TRIAL_DEV] + signs * halves[TRIAL_DEV:]) * (1.0 / math.sqrt(block_len))
    spectra = spectra.astype(jnp.bfloat16).astype(jnp.float32)

    sublanes = lax.broadcasted_iota(jnp.int32, (8, block_len), 0)
    zeros = jnp.zeros((8, half_len), jnp.float32)
    taps = []
    for trial in range(TRIAL_DEV):
        windows = []
        for first in (0, half_len):
            row = spectra[trial : trial + 1, first : first + half_len]
            wide = jnp.concatenate([zeros, jnp.broadcast_to(row, (8, half_len))], axis=1)
            for steps in (1, 2, 4):
                wide = jnp.where(sublanes & steps != 0, shift_left(wide, steps), wide)
            for start in range(0, block_len, 8):
                windows.append((shift_left(wide, start) if start else wide)[:, :half_len])
        taps.append(jnp.concatenate(windows, axis=0).astype(jnp.bfloat16))
    windows = jnp.concatenate(taps, axis=1)

    real = kernels_ref[0]
    imag = kernels_ref[1]
    weights = jnp.concatenate(
        [jnp.concatenate([real, -imag], axis=1), jnp.concatenate([imag, real], axis=1)], axis=0
    )
    correlation = jnp.dot(weights, windows, preferred_element_type=jnp.float32)
    accels = real.shape[0]
    power = correlation[:accels] * correlation[:accels] + correlation[accels:] * correlation[accels:]
    for trial in range(TRIAL_DEV):
        out_ref[:, trial, :] = power[:, trial * half_len : (trial + 1) * half_len].astype(
            jnp.bfloat16
        )


def shards(tm_count, chan_count, filterbank, chan_delay, tail_len, kernels):
    channels, block_len = filterbank.shape
    trials = tail_len.shape[0]
    accels = kernels.shape[1]
    devices = tm_count * chan_count
    parts = pl.pallas_call(
        functools.partial(partial_series, tm_count, chan_count),
        out_shape=jax.ShapeDtypeStruct((devices * ROWS, LANES), jnp.bfloat16),
        in_specs=[pl.BlockSpec(memory_space=pltpu.HBM)] * 3,
        scratch_shapes=[
            pltpu.VMEM((channels, block_len), jnp.bfloat16),
            pltpu.VMEM((chan_count, channels), jnp.int32),
            pltpu.VMEM((1, trials), jnp.int32),
            pltpu.VMEM((block_len + 3 * STEP, channels), jnp.float32),
            pltpu.VMEM((block_len + 2 * STEP, STEP * channels), jnp.bfloat16),
            pltpu.VMEM((STEP * channels, block_len // STEP * trials), jnp.bfloat16),
            pltpu.VMEM((2 * block_len, max(LANES, trials)), jnp.float32),
            pltpu.SemaphoreType.DMA((3,)),
        ],
        compiler_params=pltpu.CompilerParams(vmem_limit_bytes=40 * 1024 * 1024),
        name="partial_series",
    )(
        *(
            pltpu.with_memory_space_constraint(value, pltpu.HBM)
            for value in (
                filterbank,
                chan_delay.reshape(chan_count, channels),
                tail_len.reshape(1, trials),
            )
        )
    )
    parts = lax.all_to_all(parts, ("tm", "chan"), 0, 0, tiled=True)
    return pl.pallas_call(
        functools.partial(accel_search, tm_count, chan_count),
        out_shape=jax.ShapeDtypeStruct((accels, TRIAL_DEV, block_len // 2), jnp.bfloat16),
        compiler_params=pltpu.CompilerParams(vmem_limit_bytes=40 * 1024 * 1024),
        name="accel_search",
    )(parts, bin_table(block_len), kernels)


def solution(mesh):
    placed = (P("chan", "tm"), P(), P(), P())
    return jax.shard_map(
        functools.partial(shards, mesh.shape["tm"], mesh.shape["chan"]),
        mesh=mesh,
        in_specs=placed,
        out_specs=P(None, "chan", "tm"),
        check_vma=False,
    )
```

```python
import functools
import math

import jax
import jax.numpy as jnp
import numpy as np
from jax import lax
from jax.experimental import pallas as pl
from jax.experimental.pallas import tpu as pltpu
from jax.sharding import PartitionSpec as P

TRIAL_DEV = 4
MAXDELAY = 4096
LANES = 128
STEP = 8
ROWS = 2 * TRIAL_DEV


def bin_table(block_len):
    half_len = block_len // 2
    samples = np.arange(half_len)
    angles = (samples[:, None] * samples[None, :] % block_len) * (2.0 * math.pi / block_len)
    table = np.concatenate([np.cos(angles), -np.sin(angles)], axis=1)
    return jnp.asarray(table.astype(np.float32), jnp.bfloat16)


def shift_left(value, steps):
    width = value.shape[1]
    return pltpu.roll(value, width - steps, 1)


def as_column(row):
    count = row.shape[1]
    rows = lax.broadcasted_iota(jnp.int32, (count, count), 0)
    columns = lax.broadcasted_iota(jnp.int32, (count, count), 1)
    return jnp.sum(jnp.where(rows == columns, row, 0.0), axis=1, keepdims=True)


def trial_blocks(value, chan_count):
    parts = []
    for owner in range(chan_count):
        rows = value[owner * TRIAL_DEV : (owner + 1) * TRIAL_DEV]
        parts += [rows[:, :LANES], rows[:, LANES:]]
    return jnp.concatenate(parts, axis=0).astype(jnp.bfloat16)


def partial_series(
    tm_count,
    chan_count,
    samples_hbm,
    delay_hbm,
    tail_hbm,
    out_ref,
    samples_ref,
    delay_ref,
    tail_ref,
    turned,
    moved,
    chosen,
    total,
    arrived,
):
    channels, block_len = samples_ref.shape
    trials = tail_ref.shape[1]
    repeats = max(1, LANES // trials)
    width = repeats * trials
    groups = block_len // (STEP * repeats)
    pair = max(1, 2 * LANES // width)
    copies = [
        pltpu.make_async_copy(source, target, arrived.at[index])
        for index, (source, target) in enumerate(
            [(delay_hbm, delay_ref), (tail_hbm, tail_ref), (samples_hbm, samples_ref)]
        )
    ]
    for copy in copies:
        copy.start()
    out_ref[...] = jnp.zeros_like(out_ref)
    copies[0].wait()
    copies[1].wait()

    delays = as_column(delay_ref[pl.ds(lax.axis_index("chan"), 1), :].astype(jnp.float32))
    tails = jnp.concatenate([tail_ref[...].astype(jnp.float32)] * repeats, axis=1)
    shifts = jnp.floor(delays * tails * (1.0 / MAXDELAY))
    columns = lax.broadcasted_iota(jnp.int32, (channels, width), 1)
    rests = (shifts - STEP * (columns // trials).astype(jnp.float32)).astype(jnp.bfloat16)
    one = jnp.ones((), jnp.bfloat16)
    zero = jnp.zeros((), jnp.bfloat16)

    def where_rest_is(value):
        return jnp.where(rests == jnp.array(value, jnp.bfloat16), one, zero)

    def choose(first):
        for fine in range(STEP):
            for group in range(first, min(first + pair, groups)):
                chosen[
                    fine * channels : (fine + 1) * channels, group * width : (group + 1) * width
                ] = where_rest_is(STEP * repeats * group + fine)

    choose(0)
    whole = where_rest_is(block_len)
    parity = jnp.where(shifts - 2.0 * jnp.floor(shifts * 0.5) == 0.0, one, -one)

    copies[2].wait()
    rows = moved.shape[0]
    turned[:STEP] = jnp.zeros((STEP, channels), jnp.float32)
    turned[STEP : STEP + block_len] = samples_ref[...].astype(jnp.float32).T
    turned[STEP + block_len :] = jnp.zeros((2 * STEP, channels), jnp.float32)
    for fine in range(STEP):
        moved[:, fine * channels : (fine + 1) * channels] = turned[fine : fine + rows].astype(
            jnp.bfloat16
        )
    unmoved = moved[:, :channels]
    whole_sums = jnp.dot(unmoved, whole, preferred_element_type=jnp.float32)
    signs = lax.broadcasted_iota(jnp.int32, (STEP, rows), 0)
    signs += lax.broadcasted_iota(jnp.int32, (STEP, rows), 1)
    nyquist_step = 0.5 / block_len
    alternating = jnp.where(signs % 2 == 0, -nyquist_step, nyquist_step).astype(jnp.bfloat16)
    nyquist = jnp.dot(alternating, unmoved, preferred_element_type=jnp.float32)
    top_bin = jnp.dot(nyquist.astype(jnp.bfloat16), parity, preferred_element_type=jnp.float32)
    top_bin = jnp.where(columns[:STEP] < trials, top_bin, 0.0)

    sublanes = lax.broadcasted_iota(jnp.int32, (STEP, width), 0)
    chunks = block_len // STEP
    for chunk in range(2 * chunks):
        start = top_bin
        if chunk < chunks:
            positions = (sublanes + chunk * STEP).astype(jnp.float32)
            start = jnp.where(positions >= block_len - tails, top_bin, 0.0)
            start += whole_sums[(chunk + 1) * STEP : (chunk + 2) * STEP]
        total[chunk * STEP : (chunk + 1) * STEP] = start
    for first in range(0, groups, pair):
        if first + pair < groups:
            choose(first + pair)
        last = min(first + pair, groups)
        sums = jnp.dot(
            moved[...], chosen[:, first * width : last * width], preferred_element_type=jnp.float32
        )
        for group in range(first, last):
            start = block_len - STEP - STEP * repeats * group
            columns_of = slice((group - first) * width, (group - first + 1) * width)
            total[start : start + block_len + STEP] += sums[: block_len + STEP, columns_of]
    turned_back = total[...].T
    series = turned_back[:trials]
    for repeat in range(1, repeats):
        series += shift_left(turned_back[repeat * trials : (repeat + 1) * trials], repeat * STEP)
    series *= 1.0 / math.sqrt(channels * chan_count)

    group_rows = chan_count * ROWS
    group = lax.axis_index("tm")
    out_ref[pl.ds(pl.multiple_of(group * group_rows, group_rows), group_rows), :] = trial_blocks(
        series[:, block_len:], chan_count
    )

    @pl.when(group > 0)
    def _():
        before = pl.multiple_of((group - 1) * group_rows, group_rows)
        out_ref[pl.ds(before, group_rows), :] = trial_blocks(series[:, :block_len], chan_count)


def accel_search(
    tm_count, chan_count, parts_ref, table_ref, reverse_ref, kernels_ref, out_ref, windows, by_kernel
):
    group_rows = chan_count * ROWS
    group = lax.axis_index("tm")
    after = lax.rem(group + 1, tm_count)
    own = parts_ref[pl.ds(pl.multiple_of(group * group_rows, group_rows), group_rows), :]
    following = parts_ref[pl.ds(pl.multiple_of(after * group_rows, group_rows), group_rows), :]
    both = own.astype(jnp.float32) + following.astype(jnp.float32)
    series = jnp.sum(both.reshape(chan_count, ROWS, LANES), axis=0).astype(jnp.bfloat16)

    half_len = LANES
    block_len = 2 * half_len
    halves = jnp.dot(series, table_ref[...], preferred_element_type=jnp.float32)
    columns = lax.broadcasted_iota(jnp.int32, (TRIAL_DEV, block_len), 1)
    signs = jnp.where(columns % 2 == 0, 1.0, -1.0)
    spectra = (halves[:TRIAL_DEV] + signs * halves[TRIAL_DEV:]) * (1.0 / math.sqrt(block_len))
    spectra = spectra.astype(jnp.bfloat16).astype(jnp.float32)

    taps = lax.broadcasted_iota(jnp.int32, (half_len, half_len), 0)
    bins = lax.broadcasted_iota(jnp.int32, (half_len, half_len), 1)
    early = bins <= taps
    zero = jnp.zeros((), jnp.bfloat16)
    for trial in range(TRIAL_DEV):
        for part in range(2):
            row = spectra[trial : trial + 1, part * half_len : (part + 1) * half_len]
            turned = pltpu.roll(
                jnp.broadcast_to(row, (half_len, half_len)), 1, 1, stride=1, stride_axis=0
            ).astype(jnp.bfloat16)
            first = part * block_len
            columns_of = slice(trial * half_len, (trial + 1) * half_len)
            windows[first : first + half_len, columns_of] = jnp.where(early, turned, zero)
            windows[first + half_len : first + block_len, columns_of] = jnp.where(
                early, zero, turned
            )

    real, imag = (
        jnp.dot(kernels_ref[part], reverse_ref[...], preferred_element_type=jnp.float32).astype(
            jnp.bfloat16
        )
        for part in range(2)
    )
    weights = jnp.concatenate(
        [jnp.concatenate([real, -imag], axis=1), jnp.concatenate([imag, real], axis=1)], axis=0
    )
    correlation = jnp.dot(weights, windows[...], preferred_element_type=jnp.float32)
    accels = real.shape[0]
    power = correlation[:accels] * correlation[:accels] + correlation[accels:] * correlation[accels:]
    for trial in range(TRIAL_DEV):
        by_kernel[pl.ds(trial, accels, stride=TRIAL_DEV), :] = power[
            :, trial * half_len : (trial + 1) * half_len
        ]
    out_ref[...] = by_kernel[...].astype(jnp.bfloat16)


def shards(tm_count, chan_count, filterbank, chan_delay, tail_len, kernels):
    channels, block_len = filterbank.shape
    trials = tail_len.shape[0]
    accels = kernels.shape[1]
    devices = tm_count * chan_count
    parts = pl.pallas_call(
        functools.partial(partial_series, tm_count, chan_count),
        out_shape=jax.ShapeDtypeStruct((devices * ROWS, LANES), jnp.bfloat16),
        in_specs=[pl.BlockSpec(memory_space=pltpu.HBM)] * 3,
        scratch_shapes=[
            pltpu.VMEM((channels, block_len), jnp.bfloat16),
            pltpu.VMEM((chan_count, channels), jnp.int32),
            pltpu.VMEM((1, trials), jnp.int32),
            pltpu.VMEM((block_len + 3 * STEP, channels), jnp.float32),
            pltpu.VMEM((block_len + 2 * STEP, STEP * channels), jnp.bfloat16),
            pltpu.VMEM((STEP * channels, block_len // STEP * trials), jnp.bfloat16),
            pltpu.VMEM((2 * block_len, max(LANES, trials)), jnp.float32),
            pltpu.SemaphoreType.DMA((3,)),
        ],
        compiler_params=pltpu.CompilerParams(vmem_limit_bytes=40 * 1024 * 1024),
        name="partial_series",
    )(
        *(
            pltpu.with_memory_space_constraint(value, pltpu.HBM)
            for value in (
                filterbank,
                chan_delay.reshape(chan_count, channels),
                tail_len.reshape(1, trials),
            )
        )
    )
    parts = lax.all_to_all(parts, ("tm", "chan"), 0, 0, tiled=True)
    reverse = jnp.asarray(np.eye(block_len, dtype=np.float32)[::-1], jnp.bfloat16)
    power = pl.pallas_call(
        functools.partial(accel_search, tm_count, chan_count),
        out_shape=jax.ShapeDtypeStruct((accels * TRIAL_DEV, block_len // 2), jnp.bfloat16),
        scratch_shapes=[
            pltpu.VMEM((2 * block_len, TRIAL_DEV * block_len // 2), jnp.bfloat16),
            pltpu.VMEM((accels * TRIAL_DEV, block_len // 2), jnp.float32),
        ],
        compiler_params=pltpu.CompilerParams(vmem_limit_bytes=40 * 1024 * 1024),
        name="accel_search",
    )(parts, bin_table(block_len), reverse, kernels)
    return power.reshape(accels, TRIAL_DEV, block_len // 2)


def solution(mesh):
    placed = (P("chan", "tm"), P(), P(), P())
    return jax.shard_map(
        functools.partial(shards, mesh.shape["tm"], mesh.shape["chan"]),
        mesh=mesh,
        in_specs=placed,
        out_specs=P(None, "chan", "tm"),
        check_vma=False,
    )
```

```python
import functools
import math

import jax
import jax.numpy as jnp
import numpy as np
from jax import lax
from jax.experimental import pallas as pl
from jax.experimental.pallas import tpu as pltpu
from jax.sharding import PartitionSpec as P

TRIAL_DEV = 4
MAXDELAY = 4096
LANES = 128
STEP = 8
ROWS = 2 * TRIAL_DEV


def bin_table(block_len):
    half_len = block_len // 2
    samples = np.arange(half_len)
    angles = (samples[:, None] * samples[None, :] % block_len) * (2.0 * math.pi / block_len)
    table = np.concatenate([np.cos(angles), -np.sin(angles)], axis=1)
    return jnp.asarray(table.astype(np.float32), jnp.bfloat16)


def shift_left(value, steps):
    width = value.shape[1]
    return pltpu.roll(value, width - steps, 1)


def as_column(row):
    count = row.shape[1]
    rows = lax.broadcasted_iota(jnp.int32, (count, count), 0)
    columns = lax.broadcasted_iota(jnp.int32, (count, count), 1)
    return jnp.sum(jnp.where(rows == columns, row, 0.0), axis=1, keepdims=True)


def trial_blocks(value, chan_count):
    parts = []
    for owner in range(chan_count):
        rows = value[owner * TRIAL_DEV : (owner + 1) * TRIAL_DEV]
        parts += [rows[:, :LANES], rows[:, LANES:]]
    return jnp.concatenate(parts, axis=0).astype(jnp.bfloat16)


def partial_series(
    tm_count,
    chan_count,
    samples_hbm,
    delay_hbm,
    tail_hbm,
    out_ref,
    samples_ref,
    delay_ref,
    tail_ref,
    turned,
    moved,
    chosen,
    total,
    arrived,
):
    channels, block_len = samples_ref.shape
    trials = tail_ref.shape[1]
    repeats = max(1, LANES // trials)
    width = repeats * trials
    groups = block_len // (STEP * repeats)
    pair = max(1, 2 * LANES // width)
    copies = [
        pltpu.make_async_copy(source, target, arrived.at[index])
        for index, (source, target) in enumerate(
            [(delay_hbm, delay_ref), (tail_hbm, tail_ref), (samples_hbm, samples_ref)]
        )
    ]
    for copy in copies:
        copy.start()
    out_ref[...] = jnp.zeros_like(out_ref)
    copies[0].wait()
    copies[1].wait()

    delays = as_column(delay_ref[pl.ds(lax.axis_index("chan"), 1), :].astype(jnp.float32))
    tails = jnp.concatenate([tail_ref[...].astype(jnp.float32)] * repeats, axis=1)
    shifts = jnp.floor(delays * tails * (1.0 / MAXDELAY))
    columns = lax.broadcasted_iota(jnp.int32, (channels, width), 1)
    repeat_of = columns // trials
    rests = (shifts - STEP * groups * repeat_of.astype(jnp.float32)).astype(jnp.bfloat16)
    one = jnp.ones((), jnp.bfloat16)
    zero = jnp.zeros((), jnp.bfloat16)

    def where_rest_is(value):
        return jnp.where(rests == jnp.array(value, jnp.bfloat16), one, zero)

    def choose(first):
        for fine in range(STEP):
            for group in range(first, min(first + pair, groups)):
                chosen[
                    fine * channels : (fine + 1) * channels, group * width : (group + 1) * width
                ] = where_rest_is(STEP * group + fine)

    choose(0)
    own_shifts = shifts[:, :trials]
    whole = jnp.where(own_shifts == block_len, one, zero)
    parity = jnp.where(own_shifts - 2.0 * jnp.floor(own_shifts * 0.5) == 0.0, one, -one)

    copies[2].wait()
    rows = moved.shape[0]
    turned[:STEP] = jnp.zeros((STEP, channels), jnp.float32)
    turned[STEP : STEP + block_len] = samples_ref[...].T.astype(jnp.float32)
    turned[STEP + block_len :] = jnp.zeros((2 * STEP, channels), jnp.float32)
    for fine in range(STEP):
        moved[:, fine * channels : (fine + 1) * channels] = turned[fine : fine + rows].astype(
            jnp.bfloat16
        )
    total[...] = jnp.zeros_like(total)
    for first in range(0, groups, pair):
        if first + pair < groups:
            choose(first + pair)
        last = min(first + pair, groups)
        sums = jnp.dot(
            moved[...], chosen[:, first * width : last * width], preferred_element_type=jnp.float32
        )
        for group in range(first, last):
            start = STEP * (groups - 1 - group)
            columns_of = slice((group - first) * width, (group - first + 1) * width)
            total[start : start + block_len + STEP] += sums[: block_len + STEP, columns_of]
    signs = lax.broadcasted_iota(jnp.int32, (block_len, block_len), 0)
    signs += lax.broadcasted_iota(jnp.int32, (block_len, block_len), 1)
    nyquist_step = 0.5 / block_len
    alternating = jnp.where(signs % 2 == 0, -nyquist_step, nyquist_step).astype(jnp.bfloat16)
    samples = samples_ref[...]
    nyquist = jnp.dot(samples, alternating, preferred_element_type=jnp.float32)
    over_channels = (((0,), (0,)), ((), ()))
    top_bin = lax.dot_general(
        parity, nyquist.astype(jnp.bfloat16), over_channels, preferred_element_type=jnp.float32
    )
    whole_block = lax.dot_general(
        whole, samples, over_channels, preferred_element_type=jnp.float32
    )
    turned_back = total[...].T
    sums_by_rest = {}
    for repeat in range(repeats):
        part = turned_back[repeat * trials : (repeat + 1) * trials]
        offset = block_len - STEP * groups * (repeat + 1)
        before = offset // LANES * LANES
        after = 2 * block_len - before - part.shape[1]
        if before:
            part = jnp.concatenate([jnp.zeros((trials, before), jnp.float32), part], axis=1)
        if after > 0:
            part = jnp.concatenate([part, jnp.zeros((trials, after), jnp.float32)], axis=1)
        part = part[:, : 2 * block_len]
        rest = offset - before
        sums_by_rest[rest] = sums_by_rest[rest] + part if rest in sums_by_rest else part
    series = sum(pltpu.roll(part, rest, 1) if rest else part for rest, part in sums_by_rest.items())
    scale = 1.0 / math.sqrt(channels * chan_count)
    positions = lax.broadcasted_iota(jnp.int32, (trials, block_len), 1)
    late = (series[:, block_len:] + top_bin) * scale
    kept = positions.astype(jnp.float32) >= block_len - as_column(tails[:, :trials])
    group = lax.axis_index("tm")
    kept = jnp.logical_and(kept, group > 0)
    early = jnp.where(kept, series[:, :block_len] + top_bin + whole_block, 0.0) * scale

    group_rows = chan_count * ROWS
    before = lax.rem(group + tm_count - 1, tm_count)
    for target, value in ((group, late), (before, early)):
        first = pl.multiple_of(target * group_rows, group_rows)
        out_ref[pl.ds(first, group_rows), :] = trial_blocks(value, chan_count)


def accel_search(
    tm_count, chan_count, parts_ref, table_ref, reverse_ref, kernels_ref, out_ref, windows, by_kernel
):
    group_rows = chan_count * ROWS
    group = lax.axis_index("tm")
    after = lax.rem(group + 1, tm_count)
    own = parts_ref[pl.ds(pl.multiple_of(group * group_rows, group_rows), group_rows), :]
    following = parts_ref[pl.ds(pl.multiple_of(after * group_rows, group_rows), group_rows), :]
    both = own.astype(jnp.float32) + following.astype(jnp.float32)
    series = jnp.sum(both.reshape(chan_count, ROWS, LANES), axis=0).astype(jnp.bfloat16)

    half_len = LANES
    block_len = 2 * half_len
    halves = jnp.dot(series, table_ref[...], preferred_element_type=jnp.float32)
    columns = lax.broadcasted_iota(jnp.int32, (TRIAL_DEV, block_len), 1)
    signs = jnp.where(columns % 2 == 0, 1.0, -1.0)
    spectra = (halves[:TRIAL_DEV] + signs * halves[TRIAL_DEV:]) * (1.0 / math.sqrt(block_len))
    spectra = spectra.astype(jnp.bfloat16).astype(jnp.float32)

    taps = lax.broadcasted_iota(jnp.int32, (half_len, half_len), 0)
    bins = lax.broadcasted_iota(jnp.int32, (half_len, half_len), 1)
    early = bins <= taps
    zero = jnp.zeros((), jnp.bfloat16)
    for trial in range(TRIAL_DEV):
        for part in range(2):
            row = spectra[trial : trial + 1, part * half_len : (part + 1) * half_len]
            turned = pltpu.roll(
                jnp.broadcast_to(row, (half_len, half_len)), 1, 1, stride=1, stride_axis=0
            ).astype(jnp.bfloat16)
            first = part * block_len
            columns_of = slice(trial * half_len, (trial + 1) * half_len)
            windows[first : first + half_len, columns_of] = jnp.where(early, turned, zero)
            windows[first + half_len : first + block_len, columns_of] = jnp.where(
                early, zero, turned
            )

    real, imag = (
        jnp.dot(kernels_ref[part], reverse_ref[...], preferred_element_type=jnp.float32).astype(
            jnp.bfloat16
        )
        for part in range(2)
    )
    weights = jnp.concatenate(
        [jnp.concatenate([real, -imag], axis=1), jnp.concatenate([imag, real], axis=1)], axis=0
    )
    correlation = jnp.dot(weights, windows[...], preferred_element_type=jnp.float32)
    accels = real.shape[0]
    power = correlation[:accels] * correlation[:accels] + correlation[accels:] * correlation[accels:]
    for trial in range(TRIAL_DEV):
        by_kernel[pl.ds(trial, accels, stride=TRIAL_DEV), :] = power[
            :, trial * half_len : (trial + 1) * half_len
        ]
    out_ref[...] = by_kernel[...].astype(jnp.bfloat16)


def shards(tm_count, chan_count, filterbank, chan_delay, tail_len, kernels):
    channels, block_len = filterbank.shape
    trials = tail_len.shape[0]
    accels = kernels.shape[1]
    devices = tm_count * chan_count
    total_rows = block_len + block_len // max(1, LANES // trials)
    total_rows = -(-total_rows // LANES) * LANES
    parts = pl.pallas_call(
        functools.partial(partial_series, tm_count, chan_count),
        out_shape=jax.ShapeDtypeStruct((devices * ROWS, LANES), jnp.bfloat16),
        in_specs=[pl.BlockSpec(memory_space=pltpu.HBM)] * 3,
        scratch_shapes=[
            pltpu.VMEM((channels, block_len), jnp.bfloat16),
            pltpu.VMEM((chan_count, channels), jnp.int32),
            pltpu.VMEM((1, trials), jnp.int32),
            pltpu.VMEM((block_len + 3 * STEP, channels), jnp.float32),
            pltpu.VMEM((block_len + 2 * STEP, STEP * channels), jnp.bfloat16),
            pltpu.VMEM((STEP * channels, block_len // STEP * trials), jnp.bfloat16),
            pltpu.VMEM((total_rows, max(LANES, trials)), jnp.float32),
            pltpu.SemaphoreType.DMA((3,)),
        ],
        compiler_params=pltpu.CompilerParams(vmem_limit_bytes=40 * 1024 * 1024),
        name="partial_series",
    )(
        *(
            pltpu.with_memory_space_constraint(value, pltpu.HBM)
            for value in (
                filterbank,
                chan_delay.reshape(chan_count, channels),
                tail_len.reshape(1, trials),
            )
        )
    )
    parts = lax.all_to_all(parts, ("tm", "chan"), 0, 0, tiled=True)
    reverse = jnp.asarray(np.eye(block_len, dtype=np.float32)[::-1], jnp.bfloat16)
    power = pl.pallas_call(
        functools.partial(accel_search, tm_count, chan_count),
        out_shape=jax.ShapeDtypeStruct((accels * TRIAL_DEV, block_len // 2), jnp.bfloat16),
        scratch_shapes=[
            pltpu.VMEM((2 * block_len, TRIAL_DEV * block_len // 2), jnp.bfloat16),
            pltpu.VMEM((accels * TRIAL_DEV, block_len // 2), jnp.float32),
        ],
        compiler_params=pltpu.CompilerParams(vmem_limit_bytes=40 * 1024 * 1024),
        name="accel_search",
    )(parts, bin_table(block_len), reverse, kernels)
    return power.reshape(accels, TRIAL_DEV, block_len // 2)


def solution(mesh):
    placed = (P("chan", "tm"), P(), P(), P())
    return jax.shard_map(
        functools.partial(shards, mesh.shape["tm"], mesh.shape["chan"]),
        mesh=mesh,
        in_specs=placed,
        out_specs=P(None, "chan", "tm"),
        check_vma=False,
    )
```

```python
import functools
import math

import jax
import jax.numpy as jnp
import numpy as np
from jax import lax
from jax.experimental import pallas as pl
from jax.experimental.pallas import tpu as pltpu
from jax.sharding import PartitionSpec as P

TRIAL_DEV = 4
MAXDELAY = 4096
LANES = 128
STEP = 8
ROWS = 2 * TRIAL_DEV


def bin_table(block_len):
    half_len = block_len // 2
    samples = np.arange(half_len)
    angles = (samples[:, None] * samples[None, :] % block_len) * (2.0 * math.pi / block_len)
    table = np.concatenate([np.cos(angles), -np.sin(angles)], axis=1)
    return jnp.asarray(table.astype(np.float32), jnp.bfloat16)


def shift_left(value, steps):
    width = value.shape[1]
    return pltpu.roll(value, width - steps, 1)


def as_column(row):
    count = row.shape[1]
    rows = lax.broadcasted_iota(jnp.int32, (count, count), 0)
    columns = lax.broadcasted_iota(jnp.int32, (count, count), 1)
    return jnp.sum(jnp.where(rows == columns, row, 0.0), axis=1, keepdims=True)


def trial_blocks(value, chan_count):
    parts = []
    for owner in range(chan_count):
        rows = value[owner * TRIAL_DEV : (owner + 1) * TRIAL_DEV]
        parts += [rows[:, :LANES], rows[:, LANES:]]
    return jnp.concatenate(parts, axis=0).astype(jnp.bfloat16)


def partial_series(
    tm_count,
    chan_count,
    samples_hbm,
    delay_hbm,
    tail_hbm,
    out_ref,
    samples_ref,
    delay_ref,
    tail_ref,
    turned,
    moved,
    chosen,
    total,
    arrived,
):
    channels, block_len = samples_ref.shape
    trials = tail_ref.shape[1]
    repeats = max(1, LANES // trials)
    width = repeats * trials
    groups = block_len // (STEP * repeats)
    pair = max(1, 2 * LANES // width)
    copies = [
        pltpu.make_async_copy(source, target, arrived.at[index])
        for index, (source, target) in enumerate(
            [(delay_hbm, delay_ref), (tail_hbm, tail_ref), (samples_hbm, samples_ref)]
        )
    ]
    for copy in copies:
        copy.start()
    out_ref[...] = jnp.zeros_like(out_ref)
    copies[0].wait()
    copies[1].wait()

    delays = as_column(delay_ref[pl.ds(lax.axis_index("chan"), 1), :].astype(jnp.float32))
    tails = jnp.concatenate([tail_ref[...].astype(jnp.float32)] * repeats, axis=1)
    shifts = jnp.floor(delays * tails * (1.0 / MAXDELAY))
    columns = lax.broadcasted_iota(jnp.int32, (channels, width), 1)
    repeat_of = columns // trials
    rests = (shifts - STEP * groups * repeat_of.astype(jnp.float32)).astype(jnp.bfloat16)
    one = jnp.ones((), jnp.bfloat16)
    zero = jnp.zeros((), jnp.bfloat16)

    def where_rest_is(value):
        return jnp.where(rests == jnp.array(value, jnp.bfloat16), one, zero)

    def choose(first):
        for fine in range(STEP):
            for group in range(first, min(first + pair, groups)):
                chosen[
                    fine * channels : (fine + 1) * channels, group * width : (group + 1) * width
                ] = where_rest_is(STEP * group + fine)

    own_shifts = shifts[:, :trials]
    whole = jnp.where(own_shifts == block_len, one, zero)
    parity = jnp.where(own_shifts - 2.0 * jnp.floor(own_shifts * 0.5) == 0.0, one, -one)

    copies[2].wait()
    rows = moved.shape[0]
    turned[:STEP] = jnp.zeros((STEP, channels), jnp.float32)
    turned[STEP : STEP + block_len] = samples_ref[...].T.astype(jnp.float32)
    turned[STEP + block_len :] = jnp.zeros((2 * STEP, channels), jnp.float32)
    for fine in range(STEP):
        moved[:, fine * channels : (fine + 1) * channels] = turned[fine : fine + rows].astype(
            jnp.bfloat16
        )
    filled = STEP * (groups - 1)
    total[:filled] = jnp.zeros((filled, width), jnp.float32)
    rest = total.shape[0] - filled - block_len - STEP
    if rest:
        total[filled + block_len + STEP :] = jnp.zeros((rest, width), jnp.float32)
    for first in range(0, groups, pair):
        choose(first)
        last = min(first + pair, groups)
        sums = jnp.dot(
            moved[...], chosen[:, first * width : last * width], preferred_element_type=jnp.float32
        )
        for group in range(first, last):
            start = STEP * (groups - 1 - group)
            columns_of = slice((group - first) * width, (group - first + 1) * width)
            rows_of = slice(start, start + block_len + STEP)
            if group == 0:
                total[rows_of] = sums[: block_len + STEP, columns_of]
            else:
                total[rows_of] += sums[: block_len + STEP, columns_of]
    signs = lax.broadcasted_iota(jnp.int32, (block_len, block_len), 0)
    signs += lax.broadcasted_iota(jnp.int32, (block_len, block_len), 1)
    nyquist_step = 0.5 / block_len
    alternating = jnp.where(signs % 2 == 0, -nyquist_step, nyquist_step).astype(jnp.bfloat16)
    samples = samples_ref[...]
    nyquist = jnp.dot(samples, alternating, preferred_element_type=jnp.float32)
    over_channels = (((0,), (0,)), ((), ()))
    top_bin = lax.dot_general(
        parity, nyquist.astype(jnp.bfloat16), over_channels, preferred_element_type=jnp.float32
    )
    whole_block = lax.dot_general(
        whole, samples, over_channels, preferred_element_type=jnp.float32
    )
    turned_back = total[...].T
    sums_by_rest = {}
    for repeat in range(repeats):
        part = turned_back[repeat * trials : (repeat + 1) * trials]
        offset = block_len - STEP * groups * (repeat + 1)
        before = offset // LANES * LANES
        after = 2 * block_len - before - part.shape[1]
        if before:
            part = jnp.concatenate([jnp.zeros((trials, before), jnp.float32), part], axis=1)
        if after > 0:
            part = jnp.concatenate([part, jnp.zeros((trials, after), jnp.float32)], axis=1)
        part = part[:, : 2 * block_len]
        rest = offset - before
        sums_by_rest[rest] = sums_by_rest[rest] + part if rest in sums_by_rest else part
    series = sum(pltpu.roll(part, rest, 1) if rest else part for rest, part in sums_by_rest.items())
    scale = 1.0 / math.sqrt(channels * chan_count)
    positions = lax.broadcasted_iota(jnp.int32, (trials, block_len), 1)
    late = (series[:, block_len:] + top_bin) * scale
    kept = positions.astype(jnp.float32) >= block_len - as_column(tails[:, :trials])
    group = lax.axis_index("tm")
    kept = jnp.logical_and(kept, group > 0)
    early = jnp.where(kept, series[:, :block_len] + top_bin + whole_block, 0.0) * scale

    group_rows = chan_count * ROWS
    before = lax.rem(group + tm_count - 1, tm_count)
    for target, value in ((group, late), (before, early))[: min(tm_count, 2)]:
        first = pl.multiple_of(target * group_rows, group_rows)
        out_ref[pl.ds(first, group_rows), :] = trial_blocks(value, chan_count)


def accel_search(
    tm_count, chan_count, parts_ref, table_ref, reverse_ref, kernels_ref, out_ref, windows, by_kernel
):
    group_rows = chan_count * ROWS
    group = lax.axis_index("tm")
    after = lax.rem(group + 1, tm_count)
    own = parts_ref[pl.ds(pl.multiple_of(group * group_rows, group_rows), group_rows), :]
    both = own.astype(jnp.float32)
    if tm_count > 1:
        following = parts_ref[pl.ds(pl.multiple_of(after * group_rows, group_rows), group_rows), :]
        both += following.astype(jnp.float32)
    series = jnp.sum(both.reshape(chan_count, ROWS, LANES), axis=0).astype(jnp.bfloat16)

    half_len = LANES
    block_len = 2 * half_len
    halves = jnp.dot(series, table_ref[...], preferred_element_type=jnp.float32)
    columns = lax.broadcasted_iota(jnp.int32, (TRIAL_DEV, block_len), 1)
    signs = jnp.where(columns % 2 == 0, 1.0, -1.0)
    spectra = (halves[:TRIAL_DEV] + signs * halves[TRIAL_DEV:]) * (1.0 / math.sqrt(block_len))
    spectra = spectra.astype(jnp.bfloat16).astype(jnp.float32)

    taps = lax.broadcasted_iota(jnp.int32, (half_len, half_len), 0)
    bins = lax.broadcasted_iota(jnp.int32, (half_len, half_len), 1)
    early = bins <= taps
    zero = jnp.zeros((), jnp.bfloat16)
    for trial in range(TRIAL_DEV):
        for part in range(2):
            row = spectra[trial : trial + 1, part * half_len : (part + 1) * half_len]
            turned = pltpu.roll(
                jnp.broadcast_to(row, (half_len, half_len)), 1, 1, stride=1, stride_axis=0
            ).astype(jnp.bfloat16)
            first = part * block_len
            columns_of = slice(trial * half_len, (trial + 1) * half_len)
            windows[first : first + half_len, columns_of] = jnp.where(early, turned, zero)
            windows[first + half_len : first + block_len, columns_of] = jnp.where(
                early, zero, turned
            )

    real, imag = (
        jnp.dot(kernels_ref[part], reverse_ref[...], preferred_element_type=jnp.float32).astype(
            jnp.bfloat16
        )
        for part in range(2)
    )
    weights = jnp.concatenate(
        [jnp.concatenate([real, -imag], axis=1), jnp.concatenate([imag, real], axis=1)], axis=0
    )
    correlation = jnp.dot(weights, windows[...], preferred_element_type=jnp.float32)
    accels = real.shape[0]
    power = correlation[:accels] * correlation[:accels] + correlation[accels:] * correlation[accels:]
    for trial in range(TRIAL_DEV):
        by_kernel[pl.ds(trial, accels, stride=TRIAL_DEV), :] = power[
            :, trial * half_len : (trial + 1) * half_len
        ]
    out_ref[...] = by_kernel[...].astype(jnp.bfloat16)


def shards(tm_count, chan_count, filterbank, chan_delay, tail_len, kernels):
    channels, block_len = filterbank.shape
    trials = tail_len.shape[0]
    accels = kernels.shape[1]
    devices = tm_count * chan_count
    total_rows = block_len + block_len // max(1, LANES // trials)
    total_rows = -(-total_rows // LANES) * LANES
    parts = pl.pallas_call(
        functools.partial(partial_series, tm_count, chan_count),
        out_shape=jax.ShapeDtypeStruct((devices * ROWS, LANES), jnp.bfloat16),
        in_specs=[pl.BlockSpec(memory_space=pltpu.HBM)] * 3,
        scratch_shapes=[
            pltpu.VMEM((channels, block_len), jnp.bfloat16),
            pltpu.VMEM((chan_count, channels), jnp.int32),
            pltpu.VMEM((1, trials), jnp.int32),
            pltpu.VMEM((block_len + 3 * STEP, channels), jnp.float32),
            pltpu.VMEM((block_len + 2 * STEP, STEP * channels), jnp.bfloat16),
            pltpu.VMEM((STEP * channels, block_len // STEP * trials), jnp.bfloat16),
            pltpu.VMEM((total_rows, max(LANES, trials)), jnp.float32),
            pltpu.SemaphoreType.DMA((3,)),
        ],
        compiler_params=pltpu.CompilerParams(vmem_limit_bytes=40 * 1024 * 1024),
        name="partial_series",
    )(
        *(
            pltpu.with_memory_space_constraint(value, pltpu.HBM)
            for value in (
                filterbank,
                chan_delay.reshape(chan_count, channels),
                tail_len.reshape(1, trials),
            )
        )
    )
    parts = lax.all_to_all(parts, ("tm", "chan"), 0, 0, tiled=True)
    reverse = jnp.asarray(np.eye(block_len, dtype=np.float32)[::-1], jnp.bfloat16)
    power = pl.pallas_call(
        functools.partial(accel_search, tm_count, chan_count),
        out_shape=jax.ShapeDtypeStruct((accels * TRIAL_DEV, block_len // 2), jnp.bfloat16),
        scratch_shapes=[
            pltpu.VMEM((2 * block_len, TRIAL_DEV * block_len // 2), jnp.bfloat16),
            pltpu.VMEM((accels * TRIAL_DEV, block_len // 2), jnp.float32),
        ],
        compiler_params=pltpu.CompilerParams(vmem_limit_bytes=40 * 1024 * 1024),
        name="accel_search",
    )(parts, bin_table(block_len), reverse, kernels)
    return power.reshape(accels, TRIAL_DEV, block_len // 2)


def solution(mesh):
    placed = (P("chan", "tm"), P(), P(), P())
    return jax.shard_map(
        functools.partial(shards, mesh.shape["tm"], mesh.shape["chan"]),
        mesh=mesh,
        in_specs=placed,
        out_specs=P(None, "chan", "tm"),
        check_vma=False,
    )
```

```python
import functools
import math

import jax
import jax.numpy as jnp
import numpy as np
from jax import lax
from jax.experimental import pallas as pl
from jax.experimental.pallas import tpu as pltpu
from jax.sharding import PartitionSpec as P

TRIAL_DEV = 4
MAXDELAY = 4096
LANES = 128
STEP = 8
ROWS = 2 * TRIAL_DEV


def bin_table(block_len):
    half_len = block_len // 2
    samples = np.arange(half_len)
    angles = (samples[:, None] * samples[None, :] % block_len) * (2.0 * math.pi / block_len)
    table = np.concatenate([np.cos(angles), -np.sin(angles)], axis=1)
    return jnp.asarray(table.astype(np.float32), jnp.bfloat16)


def shift_left(value, steps):
    width = value.shape[1]
    return pltpu.roll(value, width - steps, 1)


def as_column(row):
    count = row.shape[1]
    rows = lax.broadcasted_iota(jnp.int32, (count, count), 0)
    columns = lax.broadcasted_iota(jnp.int32, (count, count), 1)
    return jnp.sum(jnp.where(rows == columns, row, 0.0), axis=1, keepdims=True)


def trial_blocks(value, chan_count):
    parts = []
    for owner in reversed(range(chan_count)):
        rows = value[owner * TRIAL_DEV : (owner + 1) * TRIAL_DEV]
        parts += [rows[:, :LANES], rows[:, LANES:]]
    return jnp.concatenate(parts, axis=0)


def group_order(tm_count, chan_count):
    groups = []
    for odd in range(1, tm_count, 2):
        for_both = sorted((odd, (odd + 1) % tm_count), reverse=True)
        groups.append(
            [block * chan_count + owner for block in for_both for owner in reversed(range(chan_count))]
        )
    return groups


def partial_series(
    chan_count,
    samples_hbm,
    delay_hbm,
    tail_hbm,
    late_ref,
    early_ref,
    samples_ref,
    delay_ref,
    tail_ref,
    turned,
    moved,
    chosen,
    total,
    arrived,
):
    channels, block_len = samples_ref.shape
    trials = tail_ref.shape[1]
    repeats = max(1, LANES // trials)
    width = repeats * trials
    groups = block_len // (STEP * repeats)
    pair = max(1, 2 * LANES // width)
    copies = [
        pltpu.make_async_copy(source, target, arrived.at[index])
        for index, (source, target) in enumerate(
            [(delay_hbm, delay_ref), (tail_hbm, tail_ref), (samples_hbm, samples_ref)]
        )
    ]
    for copy in copies:
        copy.start()
    copies[0].wait()
    copies[1].wait()

    delays = as_column(delay_ref[pl.ds(lax.axis_index("chan"), 1), :].astype(jnp.float32))
    tails = jnp.concatenate([tail_ref[...].astype(jnp.float32)] * repeats, axis=1)
    shifts = jnp.floor(delays * tails * (1.0 / MAXDELAY))
    columns = lax.broadcasted_iota(jnp.int32, (channels, width), 1)
    repeat_of = columns // trials
    rests = (shifts - STEP * groups * repeat_of.astype(jnp.float32)).astype(jnp.bfloat16)
    one = jnp.ones((), jnp.bfloat16)
    zero = jnp.zeros((), jnp.bfloat16)

    def where_rest_is(value):
        return jnp.where(rests == jnp.array(value, jnp.bfloat16), one, zero)

    def choose(first):
        for fine in range(STEP):
            for group in range(first, min(first + pair, groups)):
                chosen[
                    fine * channels : (fine + 1) * channels, group * width : (group + 1) * width
                ] = where_rest_is(STEP * group + fine)

    own_shifts = shifts[:, :trials]
    whole = jnp.where(own_shifts == block_len, one, zero)
    parity = jnp.where(own_shifts - 2.0 * jnp.floor(own_shifts * 0.5) == 0.0, one, -one)

    copies[2].wait()
    rows = moved.shape[0]
    turned[:STEP] = jnp.zeros((STEP, channels), jnp.float32)
    turned[STEP : STEP + block_len] = samples_ref[...].T.astype(jnp.float32)
    turned[STEP + block_len :] = jnp.zeros((2 * STEP, channels), jnp.float32)
    for fine in range(STEP):
        moved[:, fine * channels : (fine + 1) * channels] = turned[fine : fine + rows].astype(
            jnp.bfloat16
        )
    filled = STEP * (groups - 1)
    total[:filled] = jnp.zeros((filled, width), jnp.float32)
    rest = total.shape[0] - filled - block_len - STEP
    if rest:
        total[filled + block_len + STEP :] = jnp.zeros((rest, width), jnp.float32)
    for first in range(0, groups, pair):
        choose(first)
        last = min(first + pair, groups)
        sums = jnp.dot(
            moved[...], chosen[:, first * width : last * width], preferred_element_type=jnp.float32
        )
        for group in range(first, last):
            start = STEP * (groups - 1 - group)
            columns_of = slice((group - first) * width, (group - first + 1) * width)
            rows_of = slice(start, start + block_len + STEP)
            if group == 0:
                total[rows_of] = sums[: block_len + STEP, columns_of]
            else:
                total[rows_of] += sums[: block_len + STEP, columns_of]
    signs = lax.broadcasted_iota(jnp.int32, (block_len, block_len), 0)
    signs += lax.broadcasted_iota(jnp.int32, (block_len, block_len), 1)
    nyquist_step = 0.5 / block_len
    alternating = jnp.where(signs % 2 == 0, -nyquist_step, nyquist_step).astype(jnp.bfloat16)
    samples = samples_ref[...]
    nyquist = jnp.dot(samples, alternating, preferred_element_type=jnp.float32)
    over_channels = (((0,), (0,)), ((), ()))
    top_bin = lax.dot_general(
        parity, nyquist.astype(jnp.bfloat16), over_channels, preferred_element_type=jnp.float32
    )
    whole_block = lax.dot_general(
        whole, samples, over_channels, preferred_element_type=jnp.float32
    )
    turned_back = total[...].T
    sums_by_rest = {}
    for repeat in range(repeats):
        part = turned_back[repeat * trials : (repeat + 1) * trials]
        offset = block_len - STEP * groups * (repeat + 1)
        before = offset // LANES * LANES
        after = 2 * block_len - before - part.shape[1]
        if before:
            part = jnp.concatenate([jnp.zeros((trials, before), jnp.float32), part], axis=1)
        if after > 0:
            part = jnp.concatenate([part, jnp.zeros((trials, after), jnp.float32)], axis=1)
        part = part[:, : 2 * block_len]
        rest = offset - before
        sums_by_rest[rest] = sums_by_rest[rest] + part if rest in sums_by_rest else part
    series = sum(pltpu.roll(part, rest, 1) if rest else part for rest, part in sums_by_rest.items())
    scale = 1.0 / math.sqrt(channels * chan_count)
    positions = lax.broadcasted_iota(jnp.int32, (trials, block_len), 1)
    late = (series[:, block_len:] + top_bin) * scale
    kept = positions.astype(jnp.float32) >= block_len - as_column(tails[:, :trials])
    early = jnp.where(kept, series[:, :block_len] + top_bin + whole_block, 0.0) * scale
    late_ref[...] = trial_blocks(late, chan_count)
    early_ref[...] = trial_blocks(early, chan_count).astype(jnp.bfloat16)


def accel_search(
    parts_ref, table_ref, reverse_ref, kernels_ref, out_ref, windows, by_kernel
):
    sources = parts_ref.shape[0] // ROWS
    parts = parts_ref[...].astype(jnp.float32).reshape(sources, ROWS, LANES)
    series = jnp.sum(parts, axis=0).astype(jnp.bfloat16)

    half_len = LANES
    block_len = 2 * half_len
    halves = jnp.dot(series, table_ref[...], preferred_element_type=jnp.float32)
    columns = lax.broadcasted_iota(jnp.int32, (TRIAL_DEV, block_len), 1)
    signs = jnp.where(columns % 2 == 0, 1.0, -1.0)
    spectra = (halves[:TRIAL_DEV] + signs * halves[TRIAL_DEV:]) * (1.0 / math.sqrt(block_len))
    spectra = spectra.astype(jnp.bfloat16).astype(jnp.float32)

    taps = lax.broadcasted_iota(jnp.int32, (half_len, half_len), 0)
    bins = lax.broadcasted_iota(jnp.int32, (half_len, half_len), 1)
    early = bins <= taps
    zero = jnp.zeros((), jnp.bfloat16)
    for trial in range(TRIAL_DEV):
        for part in range(2):
            row = spectra[trial : trial + 1, part * half_len : (part + 1) * half_len]
            turned = pltpu.roll(
                jnp.broadcast_to(row, (half_len, half_len)), 1, 1, stride=1, stride_axis=0
            ).astype(jnp.bfloat16)
            first = part * block_len
            columns_of = slice(trial * half_len, (trial + 1) * half_len)
            windows[first : first + half_len, columns_of] = jnp.where(early, turned, zero)
            windows[first + half_len : first + block_len, columns_of] = jnp.where(
                early, zero, turned
            )

    real, imag = (
        jnp.dot(kernels_ref[part], reverse_ref[...], preferred_element_type=jnp.float32).astype(
            jnp.bfloat16
        )
        for part in range(2)
    )
    weights = jnp.concatenate(
        [jnp.concatenate([real, -imag], axis=1), jnp.concatenate([imag, real], axis=1)], axis=0
    )
    correlation = jnp.dot(weights, windows[...], preferred_element_type=jnp.float32)
    accels = real.shape[0]
    power = correlation[:accels] * correlation[:accels] + correlation[accels:] * correlation[accels:]
    for trial in range(TRIAL_DEV):
        by_kernel[pl.ds(trial, accels, stride=TRIAL_DEV), :] = power[
            :, trial * half_len : (trial + 1) * half_len
        ]
    out_ref[...] = by_kernel[...].astype(jnp.bfloat16)


def shards(tm_count, chan_count, filterbank, chan_delay, tail_len, kernels):
    channels, block_len = filterbank.shape
    trials = tail_len.shape[0]
    accels = kernels.shape[1]
    total_rows = block_len + block_len // max(1, LANES // trials)
    total_rows = -(-total_rows // LANES) * LANES
    group_rows = chan_count * ROWS
    late, early = pl.pallas_call(
        functools.partial(partial_series, chan_count),
        out_shape=(
            jax.ShapeDtypeStruct((group_rows, LANES), jnp.float32),
            jax.ShapeDtypeStruct((group_rows, LANES), jnp.bfloat16),
        ),
        in_specs=[pl.BlockSpec(memory_space=pltpu.HBM)] * 3,
        scratch_shapes=[
            pltpu.VMEM((channels, block_len), jnp.bfloat16),
            pltpu.VMEM((chan_count, channels), jnp.int32),
            pltpu.VMEM((1, trials), jnp.int32),
            pltpu.VMEM((block_len + 3 * STEP, channels), jnp.float32),
            pltpu.VMEM((block_len + 2 * STEP, STEP * channels), jnp.bfloat16),
            pltpu.VMEM((STEP * channels, block_len // STEP * trials), jnp.bfloat16),
            pltpu.VMEM((total_rows, max(LANES, trials)), jnp.float32),
            pltpu.SemaphoreType.DMA((3,)),
        ],
        compiler_params=pltpu.CompilerParams(vmem_limit_bytes=40 * 1024 * 1024),
        name="partial_series",
    )(
        *(
            pltpu.with_memory_space_constraint(value, pltpu.HBM)
            for value in (
                filterbank,
                chan_delay.reshape(chan_count, channels),
                tail_len.reshape(1, trials),
            )
        )
    )
    block = lax.axis_index("tm")
    is_even = block % 2 == 0
    tails = lax.ppermute(early, "tm", [(index, index ^ 1) for index in range(tm_count)])
    own = (late + jnp.where(is_even, tails.astype(jnp.float32), 0.0)).astype(jnp.bfloat16)
    other = jnp.where(jnp.logical_and(is_even, block > 0), early, jnp.zeros_like(early))
    own_first = jnp.where(is_even, block > 0, block == tm_count - 1)
    parts = jnp.concatenate(
        [jnp.where(own_first, own, other), jnp.where(own_first, other, own)], axis=0
    )
    parts = lax.all_to_all(
        parts,
        ("tm", "chan"),
        0,
        0,
        axis_index_groups=group_order(tm_count, chan_count),
        tiled=True,
    )
    reverse = jnp.asarray(np.eye(block_len, dtype=np.float32)[::-1], jnp.bfloat16)
    power = pl.pallas_call(
        accel_search,
        out_shape=jax.ShapeDtypeStruct((accels * TRIAL_DEV, block_len // 2), jnp.bfloat16),
        scratch_shapes=[
            pltpu.VMEM((2 * block_len, TRIAL_DEV * block_len // 2), jnp.bfloat16),
            pltpu.VMEM((accels * TRIAL_DEV, block_len // 2), jnp.float32),
        ],
        compiler_params=pltpu.CompilerParams(vmem_limit_bytes=40 * 1024 * 1024),
        name="accel_search",
    )(parts, bin_table(block_len), reverse, kernels)
    return power.reshape(accels, TRIAL_DEV, block_len // 2)


def solution(mesh):
    placed = (P("chan", "tm"), P(), P(), P())
    return jax.shard_map(
        functools.partial(shards, mesh.shape["tm"], mesh.shape["chan"]),
        mesh=mesh,
        in_specs=placed,
        out_specs=P(None, "chan", "tm"),
        check_vma=False,
    )
```

```python
import functools
import math

import jax
import jax.numpy as jnp
import numpy as np
from jax import lax
from jax.experimental import pallas as pl
from jax.experimental.pallas import tpu as pltpu
from jax.sharding import PartitionSpec as P

TRIAL_DEV = 4
MAXDELAY = 4096
LANES = 128
STEP = 8
ROWS = 2 * TRIAL_DEV


def bin_table(block_len):
    half_len = block_len // 2
    samples = np.arange(half_len)
    angles = (samples[:, None] * samples[None, :] % block_len) * (2.0 * math.pi / block_len)
    table = np.concatenate([np.cos(angles), -np.sin(angles)], axis=1)
    return jnp.asarray(table.astype(np.float32), jnp.bfloat16)


def shift_left(value, steps):
    width = value.shape[1]
    return pltpu.roll(value, width - steps, 1)


def as_column(row):
    count = row.shape[1]
    rows = lax.broadcasted_iota(jnp.int32, (count, count), 0)
    columns = lax.broadcasted_iota(jnp.int32, (count, count), 1)
    return jnp.sum(jnp.where(rows == columns, row, 0.0), axis=1, keepdims=True)


def chan_order(chan_count):
    return [chan_count - 1] + list(range(chan_count - 1))


def trial_blocks(value, chan_count):
    parts = []
    for owner in chan_order(chan_count):
        rows = value[owner * TRIAL_DEV : (owner + 1) * TRIAL_DEV]
        parts += [rows[:, :LANES], rows[:, LANES:]]
    return jnp.concatenate(parts, axis=0)


def group_order(tm_count, chan_count):
    groups = []
    for odd in range(1, tm_count, 2):
        blocks = sorted((odd, (odd + 1) % tm_count))
        groups.append(
            [block * chan_count + owner for block in blocks for owner in chan_order(chan_count)]
        )
    return groups


def partial_series(
    chan_count,
    samples_hbm,
    delay_hbm,
    tail_hbm,
    late_ref,
    early_ref,
    samples_ref,
    delay_ref,
    tail_ref,
    turned,
    moved,
    chosen,
    total,
    arrived,
):
    channels, block_len = samples_ref.shape
    trials = tail_ref.shape[1]
    repeats = max(1, LANES // trials)
    width = repeats * trials
    groups = block_len // (STEP * repeats)
    pair = max(1, 2 * LANES // width)
    copies = [
        pltpu.make_async_copy(source, target, arrived.at[index])
        for index, (source, target) in enumerate(
            [(delay_hbm, delay_ref), (tail_hbm, tail_ref), (samples_hbm, samples_ref)]
        )
    ]
    for copy in copies:
        copy.start()
    copies[0].wait()
    copies[1].wait()

    delays = as_column(delay_ref[pl.ds(lax.axis_index("chan"), 1), :].astype(jnp.float32))
    tails = jnp.concatenate([tail_ref[...].astype(jnp.float32)] * repeats, axis=1)
    shifts = jnp.floor(delays * tails * (1.0 / MAXDELAY))
    columns = lax.broadcasted_iota(jnp.int32, (channels, width), 1)
    repeat_of = columns // trials
    rests = (shifts - STEP * groups * repeat_of.astype(jnp.float32)).astype(jnp.bfloat16)
    one = jnp.ones((), jnp.bfloat16)
    zero = jnp.zeros((), jnp.bfloat16)

    def where_rest_is(value):
        return jnp.where(rests == jnp.array(value, jnp.bfloat16), one, zero)

    def choose(first):
        for fine in range(STEP):
            for group in range(first, min(first + pair, groups)):
                chosen[
                    fine * channels : (fine + 1) * channels, group * width : (group + 1) * width
                ] = where_rest_is(STEP * group + fine)

    own_shifts = shifts[:, :trials]
    whole = jnp.where(own_shifts == block_len, one, zero)
    parity = jnp.where(own_shifts - 2.0 * jnp.floor(own_shifts * 0.5) == 0.0, one, -one)

    copies[2].wait()
    rows = moved.shape[0]
    turned[:STEP] = jnp.zeros((STEP, channels), jnp.float32)
    turned[STEP : STEP + block_len] = samples_ref[...].T.astype(jnp.float32)
    turned[STEP + block_len :] = jnp.zeros((2 * STEP, channels), jnp.float32)
    for fine in range(STEP):
        moved[:, fine * channels : (fine + 1) * channels] = turned[fine : fine + rows].astype(
            jnp.bfloat16
        )
    filled = STEP * (groups - 1)
    total[:filled] = jnp.zeros((filled, width), jnp.float32)
    rest = total.shape[0] - filled - block_len - STEP
    if rest:
        total[filled + block_len + STEP :] = jnp.zeros((rest, width), jnp.float32)
    for first in range(0, groups, pair):
        choose(first)
        last = min(first + pair, groups)
        sums = jnp.dot(
            moved[...], chosen[:, first * width : last * width], preferred_element_type=jnp.float32
        )
        for group in range(first, last):
            start = STEP * (groups - 1 - group)
            columns_of = slice((group - first) * width, (group - first + 1) * width)
            rows_of = slice(start, start + block_len + STEP)
            if group == 0:
                total[rows_of] = sums[: block_len + STEP, columns_of]
            else:
                total[rows_of] += sums[: block_len + STEP, columns_of]
    signs = lax.broadcasted_iota(jnp.int32, (block_len, block_len), 0)
    signs += lax.broadcasted_iota(jnp.int32, (block_len, block_len), 1)
    nyquist_step = 0.5 / block_len
    alternating = jnp.where(signs % 2 == 0, -nyquist_step, nyquist_step).astype(jnp.bfloat16)
    samples = samples_ref[...]
    nyquist = jnp.dot(samples, alternating, preferred_element_type=jnp.float32)
    over_channels = (((0,), (0,)), ((), ()))
    top_bin = lax.dot_general(
        parity, nyquist.astype(jnp.bfloat16), over_channels, preferred_element_type=jnp.float32
    )
    whole_block = lax.dot_general(
        whole, samples, over_channels, preferred_element_type=jnp.float32
    )
    turned_back = total[...].T
    sums_by_rest = {}
    for repeat in range(repeats):
        part = turned_back[repeat * trials : (repeat + 1) * trials]
        offset = block_len - STEP * groups * (repeat + 1)
        before = offset // LANES * LANES
        after = 2 * block_len - before - part.shape[1]
        if before:
            part = jnp.concatenate([jnp.zeros((trials, before), jnp.float32), part], axis=1)
        if after > 0:
            part = jnp.concatenate([part, jnp.zeros((trials, after), jnp.float32)], axis=1)
        part = part[:, : 2 * block_len]
        rest = offset - before
        sums_by_rest[rest] = sums_by_rest[rest] + part if rest in sums_by_rest else part
    series = sum(pltpu.roll(part, rest, 1) if rest else part for rest, part in sums_by_rest.items())
    scale = 1.0 / math.sqrt(channels * chan_count)
    positions = lax.broadcasted_iota(jnp.int32, (trials, block_len), 1)
    late = (series[:, block_len:] + top_bin) * scale
    kept = positions.astype(jnp.float32) >= block_len - as_column(tails[:, :trials])
    early = jnp.where(kept, series[:, :block_len] + top_bin + whole_block, 0.0) * scale
    late_ref[...] = trial_blocks(late, chan_count)
    early_ref[...] = trial_blocks(early, chan_count).astype(jnp.bfloat16)


def accel_search(
    parts_ref, table_ref, reverse_ref, kernels_ref, out_ref, windows, by_kernel
):
    sources = parts_ref.shape[0] // ROWS
    parts = parts_ref[...].astype(jnp.float32).reshape(sources, ROWS, LANES)
    series = jnp.sum(parts, axis=0).astype(jnp.bfloat16)

    half_len = LANES
    block_len = 2 * half_len
    halves = jnp.dot(series, table_ref[...], preferred_element_type=jnp.float32)
    columns = lax.broadcasted_iota(jnp.int32, (TRIAL_DEV, block_len), 1)
    signs = jnp.where(columns % 2 == 0, 1.0, -1.0)
    spectra = (halves[:TRIAL_DEV] + signs * halves[TRIAL_DEV:]) * (1.0 / math.sqrt(block_len))
    spectra = spectra.astype(jnp.bfloat16).astype(jnp.float32)

    taps = lax.broadcasted_iota(jnp.int32, (half_len, half_len), 0)
    bins = lax.broadcasted_iota(jnp.int32, (half_len, half_len), 1)
    early = bins <= taps
    zero = jnp.zeros((), jnp.bfloat16)
    for trial in range(TRIAL_DEV):
        for part in range(2):
            row = spectra[trial : trial + 1, part * half_len : (part + 1) * half_len]
            turned = pltpu.roll(
                jnp.broadcast_to(row, (half_len, half_len)), 1, 1, stride=1, stride_axis=0
            ).astype(jnp.bfloat16)
            first = part * block_len
            columns_of = slice(trial * half_len, (trial + 1) * half_len)
            windows[first : first + half_len, columns_of] = jnp.where(early, turned, zero)
            windows[first + half_len : first + block_len, columns_of] = jnp.where(
                early, zero, turned
            )

    real, imag = (
        jnp.dot(kernels_ref[part], reverse_ref[...], preferred_element_type=jnp.float32).astype(
            jnp.bfloat16
        )
        for part in range(2)
    )
    weights = jnp.concatenate(
        [jnp.concatenate([real, -imag], axis=1), jnp.concatenate([imag, real], axis=1)], axis=0
    )
    correlation = jnp.dot(weights, windows[...], preferred_element_type=jnp.float32)
    accels = real.shape[0]
    power = correlation[:accels] * correlation[:accels] + correlation[accels:] * correlation[accels:]
    for trial in range(TRIAL_DEV):
        by_kernel[pl.ds(trial, accels, stride=TRIAL_DEV), :] = power[
            :, trial * half_len : (trial + 1) * half_len
        ]
    out_ref[...] = by_kernel[...].astype(jnp.bfloat16)


def shards(tm_count, chan_count, filterbank, chan_delay, tail_len, kernels):
    channels, block_len = filterbank.shape
    trials = tail_len.shape[0]
    accels = kernels.shape[1]
    total_rows = block_len + block_len // max(1, LANES // trials)
    total_rows = -(-total_rows // LANES) * LANES
    group_rows = chan_count * ROWS
    late, early = pl.pallas_call(
        functools.partial(partial_series, chan_count),
        out_shape=(
            jax.ShapeDtypeStruct((group_rows, LANES), jnp.float32),
            jax.ShapeDtypeStruct((group_rows, LANES), jnp.bfloat16),
        ),
        in_specs=[pl.BlockSpec(memory_space=pltpu.HBM)] * 3,
        scratch_shapes=[
            pltpu.VMEM((channels, block_len), jnp.bfloat16),
            pltpu.VMEM((chan_count, channels), jnp.int32),
            pltpu.VMEM((1, trials), jnp.int32),
            pltpu.VMEM((block_len + 3 * STEP, channels), jnp.float32),
            pltpu.VMEM((block_len + 2 * STEP, STEP * channels), jnp.bfloat16),
            pltpu.VMEM((STEP * channels, block_len // STEP * trials), jnp.bfloat16),
            pltpu.VMEM((total_rows, max(LANES, trials)), jnp.float32),
            pltpu.SemaphoreType.DMA((3,)),
        ],
        compiler_params=pltpu.CompilerParams(vmem_limit_bytes=40 * 1024 * 1024),
        name="partial_series",
    )(
        *(
            pltpu.with_memory_space_constraint(value, pltpu.HBM)
            for value in (
                filterbank,
                chan_delay.reshape(chan_count, channels),
                tail_len.reshape(1, trials),
            )
        )
    )
    block = lax.axis_index("tm")
    is_even = block % 2 == 0
    tails = lax.ppermute(early, "tm", [(index, index ^ 1) for index in range(tm_count)])
    own = (late + jnp.where(is_even, tails.astype(jnp.float32), 0.0)).astype(jnp.bfloat16)
    other = jnp.where(jnp.logical_and(is_even, block > 0), early, jnp.zeros_like(early))
    own_first = jnp.where(is_even, block == 0, block < tm_count - 1)
    parts = jnp.concatenate(
        [jnp.where(own_first, own, other), jnp.where(own_first, other, own)], axis=0
    )
    parts = lax.all_to_all(
        parts,
        ("tm", "chan"),
        0,
        0,
        axis_index_groups=group_order(tm_count, chan_count),
        tiled=True,
    )
    reverse = jnp.asarray(np.eye(block_len, dtype=np.float32)[::-1], jnp.bfloat16)
    power = pl.pallas_call(
        accel_search,
        out_shape=jax.ShapeDtypeStruct((accels * TRIAL_DEV, block_len // 2), jnp.bfloat16),
        scratch_shapes=[
            pltpu.VMEM((2 * block_len, TRIAL_DEV * block_len // 2), jnp.bfloat16),
            pltpu.VMEM((accels * TRIAL_DEV, block_len // 2), jnp.float32),
        ],
        compiler_params=pltpu.CompilerParams(vmem_limit_bytes=40 * 1024 * 1024),
        name="accel_search",
    )(parts, bin_table(block_len), reverse, kernels)
    return power.reshape(accels, TRIAL_DEV, block_len // 2)


def solution(mesh):
    placed = (P("chan", "tm"), P(), P(), P())
    return jax.shard_map(
        functools.partial(shards, mesh.shape["tm"], mesh.shape["chan"]),
        mesh=mesh,
        in_specs=placed,
        out_specs=P(None, "chan", "tm"),
        check_vma=False,
    )
```

```python
import functools
import math

import jax
import jax.numpy as jnp
import numpy as np
from jax import lax
from jax.experimental import pallas as pl
from jax.experimental.pallas import tpu as pltpu
from jax.sharding import PartitionSpec as P

TRIAL_DEV = 4
MAXDELAY = 4096
LANES = 128
STEP = 8
ROWS = 2 * TRIAL_DEV


def bin_table(block_len):
    half_len = block_len // 2
    samples = np.arange(half_len)
    angles = (samples[:, None] * samples[None, :] % block_len) * (2.0 * math.pi / block_len)
    table = np.concatenate([np.cos(angles), -np.sin(angles)], axis=1)
    return jnp.asarray(table.astype(np.float32), jnp.bfloat16)


def shift_left(value, steps):
    width = value.shape[1]
    return pltpu.roll(value, width - steps, 1)


def as_column(row):
    count = row.shape[1]
    rows = lax.broadcasted_iota(jnp.int32, (count, count), 0)
    columns = lax.broadcasted_iota(jnp.int32, (count, count), 1)
    return jnp.sum(jnp.where(rows == columns, row, 0.0), axis=1, keepdims=True)


def chan_order(chan_count):
    return [chan_count - 1] + list(range(chan_count - 1))


def trial_blocks(value, chan_count):
    parts = []
    for owner in chan_order(chan_count):
        rows = value[owner * TRIAL_DEV : (owner + 1) * TRIAL_DEV]
        parts += [rows[:, :LANES], rows[:, LANES:]]
    return jnp.concatenate(parts, axis=0)


def group_order(tm_count, chan_count):
    groups = []
    for odd in range(1, tm_count, 2):
        blocks = sorted((odd, (odd + 1) % tm_count))
        groups.append(
            [block * chan_count + owner for block in blocks for owner in chan_order(chan_count)]
        )
    return groups


def fold(total, trials, block_len):
    width = total.shape[1]
    repeats = width // trials
    repeat_of = lax.broadcasted_iota(jnp.int32, (block_len, width), 1) // trials
    sums = total[:block_len]
    for repeat in range(1, repeats):
        first = repeat * STEP
        sums = jnp.where(repeat_of == repeat, total[first : first + block_len], sums)
    turned_back = sums.T
    return sum(turned_back[repeat * trials : (repeat + 1) * trials] for repeat in range(repeats))


def partial_series(
    chan_count,
    samples_hbm,
    delay_hbm,
    tail_hbm,
    early_ref,
    moved,
    chosen,
    top_bin_ref,
    samples_ref,
    delay_ref,
    tail_ref,
    turned,
    total,
    arrived,
):
    channels, block_len = samples_ref.shape
    trials = tail_ref.shape[1]
    repeats = max(1, LANES // trials)
    width = repeats * trials
    groups = block_len // (STEP * repeats)
    pair = max(1, 2 * LANES // width)
    copies = [
        pltpu.make_async_copy(source, target, arrived.at[index])
        for index, (source, target) in enumerate(
            [(delay_hbm, delay_ref), (tail_hbm, tail_ref), (samples_hbm, samples_ref)]
        )
    ]
    for copy in copies:
        copy.start()
    copies[0].wait()
    copies[1].wait()

    delays = as_column(delay_ref[pl.ds(lax.axis_index("chan"), 1), :].astype(jnp.float32))
    tails = jnp.concatenate([tail_ref[...].astype(jnp.float32)] * repeats, axis=1)
    shifts = jnp.floor(delays * tails * (1.0 / MAXDELAY))
    columns = lax.broadcasted_iota(jnp.int32, (channels, width), 1)
    repeat_of = columns // trials
    rests = (shifts - STEP * repeat_of.astype(jnp.float32)).astype(jnp.bfloat16)
    one = jnp.ones((), jnp.bfloat16)
    zero = jnp.zeros((), jnp.bfloat16)

    def where_rest_is(value):
        return jnp.where(rests == jnp.array(value, jnp.bfloat16), one, zero)

    def choose(first):
        for fine in range(STEP):
            for group in range(first, min(first + pair, groups)):
                chosen[
                    fine * channels : (fine + 1) * channels, group * width : (group + 1) * width
                ] = where_rest_is(STEP * repeats * group + fine)

    own_shifts = shifts[:, :trials]
    whole = jnp.where(own_shifts == block_len, one, zero)
    parity = jnp.where(own_shifts - 2.0 * jnp.floor(own_shifts * 0.5) == 0.0, one, -one)

    copies[2].wait()
    rows = moved.shape[0]
    turned[:STEP] = jnp.zeros((STEP, channels), jnp.float32)
    turned[STEP : STEP + block_len] = samples_ref[...].T.astype(jnp.float32)
    turned[STEP + block_len :] = jnp.zeros((2 * STEP, channels), jnp.float32)
    for fine in range(STEP):
        moved[:, fine * channels : (fine + 1) * channels] = turned[fine : fine + rows].astype(
            jnp.bfloat16
        )
    step = STEP * repeats
    end = block_len + step - STEP
    total[...] = jnp.zeros_like(total)
    firsts = list(range(0, groups, pair))
    half = len(firsts) // 2
    for first in firsts[half:][::-1] + firsts[:half]:
        choose(first)
        last = min(first + pair, groups)
        sums = jnp.dot(
            moved[: step * last],
            chosen[:, first * width : last * width],
            preferred_element_type=jnp.float32,
        )
        for group in range(first, last):
            columns_of = slice((group - first) * width, (group - first + 1) * width)
            total[end - step * (group + 1) : end] += sums[: step * (group + 1), columns_of]
    signs = lax.broadcasted_iota(jnp.int32, (block_len, block_len), 0)
    signs += lax.broadcasted_iota(jnp.int32, (block_len, block_len), 1)
    nyquist_step = 0.5 / block_len
    alternating = jnp.where(signs % 2 == 0, -nyquist_step, nyquist_step).astype(jnp.bfloat16)
    samples = samples_ref[...]
    nyquist = jnp.dot(samples, alternating, preferred_element_type=jnp.float32)
    over_channels = (((0,), (0,)), ((), ()))
    top_bin = lax.dot_general(
        parity, nyquist.astype(jnp.bfloat16), over_channels, preferred_element_type=jnp.float32
    )
    whole_block = lax.dot_general(
        whole, samples, over_channels, preferred_element_type=jnp.float32
    )
    early = fold(total, trials, block_len) + top_bin + whole_block
    positions = lax.broadcasted_iota(jnp.int32, (trials, block_len), 1)
    kept = positions.astype(jnp.float32) >= block_len - as_column(tails[:, :trials])
    early = jnp.where(kept, early, 0.0) * (1.0 / math.sqrt(channels * chan_count))
    early_ref[...] = trial_blocks(early, chan_count).astype(jnp.bfloat16)
    top_bin_ref[...] = top_bin


def late_series(chan_count, scale, moved, chosen, top_bin_ref, late_ref, total):
    trials, block_len = top_bin_ref.shape
    repeats = max(1, LANES // trials)
    width = repeats * trials
    step = STEP * repeats
    groups = block_len // step
    pair = max(1, 2 * LANES // width)
    total[...] = jnp.zeros_like(total)
    for first in range(0, groups, pair):
        last = min(first + pair, groups)
        start = step * first
        sums = jnp.dot(
            moved[start:], chosen[:, first * width : last * width], preferred_element_type=jnp.float32
        )
        for group in range(first, last):
            columns_of = slice((group - first) * width, (group - first + 1) * width)
            rows_of = slice(step * group + STEP - start, block_len + STEP - start)
            total[: block_len - step * group] += sums[rows_of, columns_of]
    late = (fold(total, trials, block_len) + top_bin_ref[...]) * scale
    late_ref[...] = trial_blocks(late, chan_count)


def accel_search(
    parts_ref, table_ref, kernels_ref, out_ref, windows, by_kernel
):
    sources = parts_ref.shape[0] // ROWS
    parts = parts_ref[...].astype(jnp.float32).reshape(sources, ROWS, LANES)
    series = jnp.sum(parts, axis=0).astype(jnp.bfloat16)

    half_len = LANES
    block_len = 2 * half_len
    halves = jnp.dot(series, table_ref[...], preferred_element_type=jnp.float32)
    columns = lax.broadcasted_iota(jnp.int32, (TRIAL_DEV, block_len), 1)
    signs = jnp.where(columns % 2 == 0, 1.0, -1.0)
    spectra = (halves[:TRIAL_DEV] + signs * halves[TRIAL_DEV:]) * (1.0 / math.sqrt(block_len))
    spectra = spectra.astype(jnp.bfloat16).astype(jnp.float32)

    taps = lax.broadcasted_iota(jnp.int32, (half_len, half_len), 0)
    bins = lax.broadcasted_iota(jnp.int32, (half_len, half_len), 1)
    early = bins <= taps
    zero = jnp.zeros((), jnp.bfloat16)
    for trial in range(TRIAL_DEV):
        for part in range(2):
            row = spectra[trial : trial + 1, part * half_len : (part + 1) * half_len]
            turned = pltpu.roll(
                jnp.broadcast_to(row, (half_len, half_len)), 1, 1, stride=1, stride_axis=0
            ).astype(jnp.bfloat16)
            first = part * block_len
            columns_of = slice(trial * half_len, (trial + 1) * half_len)
            windows[first : first + half_len, columns_of] = jnp.where(early, turned, zero)
            windows[first + half_len : first + block_len, columns_of] = jnp.where(
                early, zero, turned
            )

    ends = lax.broadcasted_iota(jnp.int32, (block_len, block_len), 0)
    ends += lax.broadcasted_iota(jnp.int32, (block_len, block_len), 1)
    reverse = jnp.where(ends == block_len - 1, 1.0, 0.0).astype(jnp.bfloat16)
    real, imag = (
        jnp.dot(kernels_ref[part], reverse, preferred_element_type=jnp.float32).astype(
            jnp.bfloat16
        )
        for part in range(2)
    )
    weights = jnp.concatenate(
        [jnp.concatenate([real, -imag], axis=1), jnp.concatenate([imag, real], axis=1)], axis=0
    )
    correlation = jnp.dot(weights, windows[...], preferred_element_type=jnp.float32)
    accels = real.shape[0]
    power = correlation[:accels] * correlation[:accels] + correlation[accels:] * correlation[accels:]
    for trial in range(TRIAL_DEV):
        by_kernel[pl.ds(trial, accels, stride=TRIAL_DEV), :] = power[
            :, trial * half_len : (trial + 1) * half_len
        ]
    out_ref[...] = by_kernel[...].astype(jnp.bfloat16)


def shards(tm_count, chan_count, filterbank, chan_delay, tail_len, kernels):
    channels, block_len = filterbank.shape
    trials = tail_len.shape[0]
    accels = kernels.shape[1]
    total_rows = block_len + STEP * (max(1, LANES // trials) - 1)
    total = pltpu.VMEM((total_rows, max(LANES, trials)), jnp.float32)
    group_rows = chan_count * ROWS
    early, moved, chosen, top_bin = pl.pallas_call(
        functools.partial(partial_series, chan_count),
        out_shape=(
            jax.ShapeDtypeStruct((group_rows, LANES), jnp.bfloat16),
            jax.ShapeDtypeStruct((block_len + 2 * STEP, STEP * channels), jnp.bfloat16),
            jax.ShapeDtypeStruct((STEP * channels, block_len // STEP * trials), jnp.bfloat16),
            jax.ShapeDtypeStruct((trials, block_len), jnp.float32),
        ),
        in_specs=[pl.BlockSpec(memory_space=pltpu.HBM)] * 3,
        scratch_shapes=[
            pltpu.VMEM((channels, block_len), jnp.bfloat16),
            pltpu.VMEM((chan_count, channels), jnp.int32),
            pltpu.VMEM((1, trials), jnp.int32),
            pltpu.VMEM((block_len + 3 * STEP, channels), jnp.float32),
            total,
            pltpu.SemaphoreType.DMA((3,)),
        ],
        compiler_params=pltpu.CompilerParams(vmem_limit_bytes=40 * 1024 * 1024),
        name="partial_series",
    )(
        *(
            pltpu.with_memory_space_constraint(value, pltpu.HBM)
            for value in (
                filterbank,
                chan_delay.reshape(chan_count, channels),
                tail_len.reshape(1, trials),
            )
        )
    )
    tails = lax.ppermute(early, "tm", [(index, index ^ 1) for index in range(tm_count)])
    late = pl.pallas_call(
        functools.partial(late_series, chan_count, 1.0 / math.sqrt(channels * chan_count)),
        out_shape=jax.ShapeDtypeStruct((group_rows, LANES), jnp.float32),
        scratch_shapes=[total],
        compiler_params=pltpu.CompilerParams(vmem_limit_bytes=16 * 1024 * 1024),
        cost_estimate=pl.CostEstimate(
            flops=2 * block_len * STEP * channels * block_len // STEP * trials,
            bytes_accessed=4 * block_len * block_len,
            transcendentals=0,
        ),
        name="late_series",
    )(moved, chosen, top_bin)
    block = lax.axis_index("tm")
    is_even = block % 2 == 0
    own = (late + jnp.where(is_even, tails.astype(jnp.float32), 0.0)).astype(jnp.bfloat16)
    other = jnp.where(jnp.logical_and(is_even, block > 0), early, jnp.zeros_like(early))
    own_first = jnp.where(is_even, block == 0, block < tm_count - 1)
    parts = jnp.concatenate(
        [jnp.where(own_first, own, other), jnp.where(own_first, other, own)], axis=0
    )
    parts = lax.all_to_all(
        parts,
        ("tm", "chan"),
        0,
        0,
        axis_index_groups=group_order(tm_count, chan_count),
        tiled=True,
    )
    power = pl.pallas_call(
        accel_search,
        out_shape=jax.ShapeDtypeStruct((accels * TRIAL_DEV, block_len // 2), jnp.bfloat16),
        scratch_shapes=[
            pltpu.VMEM((2 * block_len, TRIAL_DEV * block_len // 2), jnp.bfloat16),
            pltpu.VMEM((accels * TRIAL_DEV, block_len // 2), jnp.float32),
        ],
        compiler_params=pltpu.CompilerParams(vmem_limit_bytes=40 * 1024 * 1024),
        name="accel_search",
    )(parts, bin_table(block_len), kernels)
    return power.reshape(accels, TRIAL_DEV, block_len // 2)


def solution(mesh):
    placed = (P("chan", "tm"), P(), P(), P())
    return jax.shard_map(
        functools.partial(shards, mesh.shape["tm"], mesh.shape["chan"]),
        mesh=mesh,
        in_specs=placed,
        out_specs=P(None, "chan", "tm"),
        check_vma=False,
    )
```

```python
import functools
import math

import jax
import jax.numpy as jnp
import numpy as np
from jax import lax
from jax.experimental import pallas as pl
from jax.experimental.pallas import tpu as pltpu
from jax.sharding import PartitionSpec as P

TRIAL_DEV = 4
MAXDELAY = 4096
LANES = 128
STEP = 8
ROWS = 2 * TRIAL_DEV


def bin_table(block_len):
    half_len = block_len // 2
    samples = np.arange(half_len)
    angles = (samples[:, None] * samples[None, :] % block_len) * (2.0 * math.pi / block_len)
    table = np.concatenate([np.cos(angles), -np.sin(angles)], axis=1)
    return jnp.asarray(table.astype(np.float32), jnp.bfloat16)


def shift_left(value, steps):
    width = value.shape[1]
    return pltpu.roll(value, width - steps, 1)


def as_column(row):
    count = row.shape[1]
    rows = lax.broadcasted_iota(jnp.int32, (count, count), 0)
    columns = lax.broadcasted_iota(jnp.int32, (count, count), 1)
    return jnp.sum(jnp.where(rows == columns, row, 0.0), axis=1, keepdims=True)


def chan_order(chan_count):
    return [chan_count - 1] + list(range(chan_count - 1))


def trial_blocks(value, chan_count):
    parts = []
    for owner in chan_order(chan_count):
        rows = value[owner * TRIAL_DEV : (owner + 1) * TRIAL_DEV]
        parts += [rows[:, :LANES], rows[:, LANES:]]
    return jnp.concatenate(parts, axis=0)


def group_order(tm_count, chan_count):
    groups = []
    for odd in range(1, tm_count, 2):
        blocks = sorted((odd, (odd + 1) % tm_count))
        groups.append(
            [block * chan_count + owner for block in blocks for owner in chan_order(chan_count)]
        )
    return groups


def fold(total, trials, block_len):
    width = total.shape[1]
    repeats = width // trials
    repeat_of = lax.broadcasted_iota(jnp.int32, (block_len, width), 1) // trials
    sums = total[:block_len]
    for repeat in range(1, repeats):
        first = repeat * STEP
        sums = jnp.where(repeat_of == repeat, total[first : first + block_len], sums)
    turned_back = sums.T
    return sum(turned_back[repeat * trials : (repeat + 1) * trials] for repeat in range(repeats))


def partial_series(
    chan_count,
    samples_hbm,
    delay_hbm,
    tail_hbm,
    early_ref,
    moved,
    chosen,
    top_bin_ref,
    samples_ref,
    delay_ref,
    tail_ref,
    turned,
    total,
    arrived,
):
    channels, block_len = samples_ref.shape
    trials = tail_ref.shape[1]
    repeats = max(1, LANES // trials)
    width = repeats * trials
    groups = block_len // (STEP * repeats)
    pair = max(1, 2 * LANES // width)
    copies = [
        pltpu.make_async_copy(source, target, arrived.at[index])
        for index, (source, target) in enumerate(
            [(delay_hbm, delay_ref), (tail_hbm, tail_ref), (samples_hbm, samples_ref)]
        )
    ]
    for copy in copies:
        copy.start()
    copies[0].wait()
    copies[1].wait()

    delays = as_column(delay_ref[pl.ds(lax.axis_index("chan"), 1), :].astype(jnp.float32))
    tails = jnp.concatenate([tail_ref[...].astype(jnp.float32)] * repeats, axis=1)
    shifts = jnp.floor(delays * tails * (1.0 / MAXDELAY))
    columns = lax.broadcasted_iota(jnp.int32, (channels, width), 1)
    repeat_of = columns // trials
    rests = (shifts - STEP * repeat_of.astype(jnp.float32)).astype(jnp.bfloat16)
    one = jnp.ones((), jnp.bfloat16)
    zero = jnp.zeros((), jnp.bfloat16)

    def where_rest_is(value):
        return jnp.where(rests == jnp.array(value, jnp.bfloat16), one, zero)

    def choose(first):
        for fine in range(STEP):
            for group in range(first, min(first + pair, groups)):
                chosen[
                    fine * channels : (fine + 1) * channels, group * width : (group + 1) * width
                ] = where_rest_is(STEP * repeats * group + fine)

    firsts = list(range(0, groups, pair))
    half = len(firsts) // 2
    firsts = firsts[half:][::-1] + firsts[:half]
    for first in firsts[:1]:
        choose(first)
    own_shifts = shifts[:, :trials]
    whole = jnp.where(own_shifts == block_len, one, zero)
    parity = jnp.where(own_shifts - 2.0 * jnp.floor(own_shifts * 0.5) == 0.0, one, -one)

    copies[2].wait()
    rows = moved.shape[0]
    turned[:STEP] = jnp.zeros((STEP, channels), jnp.float32)
    turned[STEP : STEP + block_len] = samples_ref[...].T.astype(jnp.float32)
    turned[STEP + block_len :] = jnp.zeros((2 * STEP, channels), jnp.float32)
    for fine in range(STEP):
        moved[:, fine * channels : (fine + 1) * channels] = turned[fine : fine + rows].astype(
            jnp.bfloat16
        )
    step = STEP * repeats
    end = block_len + step - STEP
    total[...] = jnp.zeros_like(total)
    for index, first in enumerate(firsts):
        if index >= 1:
            choose(first)
        last = min(first + pair, groups)
        sums = jnp.dot(
            moved[: step * last],
            chosen[:, first * width : last * width],
            preferred_element_type=jnp.float32,
        )
        for group in range(first, last):
            columns_of = slice((group - first) * width, (group - first + 1) * width)
            total[end - step * (group + 1) : end] += sums[: step * (group + 1), columns_of]
    signs = lax.broadcasted_iota(jnp.int32, (block_len, block_len), 0)
    signs += lax.broadcasted_iota(jnp.int32, (block_len, block_len), 1)
    nyquist_step = 0.5 / block_len
    alternating = jnp.where(signs % 2 == 0, -nyquist_step, nyquist_step).astype(jnp.bfloat16)
    samples = samples_ref[...]
    nyquist = jnp.dot(samples, alternating, preferred_element_type=jnp.float32)
    over_channels = (((0,), (0,)), ((), ()))
    top_bin = lax.dot_general(
        parity, nyquist.astype(jnp.bfloat16), over_channels, preferred_element_type=jnp.float32
    )
    whole_block = lax.dot_general(
        whole, samples, over_channels, preferred_element_type=jnp.float32
    )
    early = fold(total, trials, block_len) + top_bin + whole_block
    positions = lax.broadcasted_iota(jnp.int32, (trials, block_len), 1)
    kept = positions.astype(jnp.float32) >= block_len - as_column(tails[:, :trials])
    early = jnp.where(kept, early, 0.0) * (1.0 / math.sqrt(channels * chan_count))
    early_ref[...] = trial_blocks(early, chan_count).astype(jnp.bfloat16)
    top_bin_ref[...] = top_bin


def late_series(chan_count, scale, moved, chosen, top_bin_ref, late_ref, total):
    trials, block_len = top_bin_ref.shape
    repeats = max(1, LANES // trials)
    width = repeats * trials
    step = STEP * repeats
    groups = block_len // step
    pair = max(1, 2 * LANES // width)
    total[...] = jnp.zeros_like(total)
    for first in range(0, groups, pair):
        last = min(first + pair, groups)
        start = step * first
        sums = jnp.dot(
            moved[start:], chosen[:, first * width : last * width], preferred_element_type=jnp.float32
        )
        for group in range(first, last):
            columns_of = slice((group - first) * width, (group - first + 1) * width)
            rows_of = slice(step * group + STEP - start, block_len + STEP - start)
            total[: block_len - step * group] += sums[rows_of, columns_of]
    late = (fold(total, trials, block_len) + top_bin_ref[...]) * scale
    late_ref[...] = trial_blocks(late, chan_count)


def accel_search(
    parts_ref, table_ref, kernels_ref, out_ref, windows, by_kernel
):
    sources = parts_ref.shape[0] // ROWS
    parts = parts_ref[...].astype(jnp.float32).reshape(sources, ROWS, LANES)
    series = jnp.sum(parts, axis=0).astype(jnp.bfloat16)

    half_len = LANES
    block_len = 2 * half_len
    halves = jnp.dot(series, table_ref[...], preferred_element_type=jnp.float32)
    columns = lax.broadcasted_iota(jnp.int32, (TRIAL_DEV, block_len), 1)
    signs = jnp.where(columns % 2 == 0, 1.0, -1.0)
    spectra = (halves[:TRIAL_DEV] + signs * halves[TRIAL_DEV:]) * (1.0 / math.sqrt(block_len))
    spectra = spectra.astype(jnp.bfloat16).astype(jnp.float32)

    taps = lax.broadcasted_iota(jnp.int32, (half_len, half_len), 0)
    bins = lax.broadcasted_iota(jnp.int32, (half_len, half_len), 1)
    early = bins <= taps
    zero = jnp.zeros((), jnp.bfloat16)
    for trial in range(TRIAL_DEV):
        for part in range(2):
            row = spectra[trial : trial + 1, part * half_len : (part + 1) * half_len]
            turned = pltpu.roll(
                jnp.broadcast_to(row, (half_len, half_len)), 1, 1, stride=1, stride_axis=0
            ).astype(jnp.bfloat16)
            first = part * block_len
            columns_of = slice(trial * half_len, (trial + 1) * half_len)
            windows[first : first + half_len, columns_of] = jnp.where(early, turned, zero)
            windows[first + half_len : first + block_len, columns_of] = jnp.where(
                early, zero, turned
            )

    ends = lax.broadcasted_iota(jnp.int32, (block_len, block_len), 0)
    ends += lax.broadcasted_iota(jnp.int32, (block_len, block_len), 1)
    reverse = jnp.where(ends == block_len - 1, 1.0, 0.0).astype(jnp.bfloat16)
    real, imag = (
        jnp.dot(kernels_ref[part], reverse, preferred_element_type=jnp.float32).astype(
            jnp.bfloat16
        )
        for part in range(2)
    )
    weights = jnp.concatenate(
        [jnp.concatenate([real, -imag], axis=1), jnp.concatenate([imag, real], axis=1)], axis=0
    )
    correlation = jnp.dot(weights, windows[...], preferred_element_type=jnp.float32)
    accels = real.shape[0]
    power = correlation[:accels] * correlation[:accels] + correlation[accels:] * correlation[accels:]
    for trial in range(TRIAL_DEV):
        by_kernel[pl.ds(trial, accels, stride=TRIAL_DEV), :] = power[
            :, trial * half_len : (trial + 1) * half_len
        ]
    out_ref[...] = by_kernel[...].astype(jnp.bfloat16)


def shards(tm_count, chan_count, filterbank, chan_delay, tail_len, kernels):
    channels, block_len = filterbank.shape
    trials = tail_len.shape[0]
    accels = kernels.shape[1]
    total_rows = block_len + STEP * (max(1, LANES // trials) - 1)
    total = pltpu.VMEM((total_rows, max(LANES, trials)), jnp.float32)
    group_rows = chan_count * ROWS
    early, moved, chosen, top_bin = pl.pallas_call(
        functools.partial(partial_series, chan_count),
        out_shape=(
            jax.ShapeDtypeStruct((group_rows, LANES), jnp.bfloat16),
            jax.ShapeDtypeStruct((block_len + 2 * STEP, STEP * channels), jnp.bfloat16),
            jax.ShapeDtypeStruct((STEP * channels, block_len // STEP * trials), jnp.bfloat16),
            jax.ShapeDtypeStruct((trials, block_len), jnp.float32),
        ),
        in_specs=[pl.BlockSpec(memory_space=pltpu.HBM)] * 3,
        scratch_shapes=[
            pltpu.VMEM((channels, block_len), jnp.bfloat16),
            pltpu.VMEM((chan_count, channels), jnp.int32),
            pltpu.VMEM((1, trials), jnp.int32),
            pltpu.VMEM((block_len + 3 * STEP, channels), jnp.float32),
            total,
            pltpu.SemaphoreType.DMA((3,)),
        ],
        compiler_params=pltpu.CompilerParams(vmem_limit_bytes=40 * 1024 * 1024),
        name="partial_series",
    )(
        *(
            pltpu.with_memory_space_constraint(value, pltpu.HBM)
            for value in (
                filterbank,
                chan_delay.reshape(chan_count, channels),
                tail_len.reshape(1, trials),
            )
        )
    )
    tails = lax.ppermute(early, "tm", [(index, index ^ 1) for index in range(tm_count)])
    late = pl.pallas_call(
        functools.partial(late_series, chan_count, 1.0 / math.sqrt(channels * chan_count)),
        out_shape=jax.ShapeDtypeStruct((group_rows, LANES), jnp.float32),
        scratch_shapes=[total],
        compiler_params=pltpu.CompilerParams(vmem_limit_bytes=16 * 1024 * 1024),
        cost_estimate=pl.CostEstimate(
            flops=2 * block_len * STEP * channels * block_len // STEP * trials,
            bytes_accessed=4 * block_len * block_len,
            transcendentals=0,
        ),
        name="late_series",
    )(moved, chosen, top_bin)
    block = lax.axis_index("tm")
    is_even = block % 2 == 0
    own = (late + jnp.where(is_even, tails.astype(jnp.float32), 0.0)).astype(jnp.bfloat16)
    other = jnp.where(jnp.logical_and(is_even, block > 0), early, jnp.zeros_like(early))
    own_first = jnp.where(is_even, block == 0, block < tm_count - 1)
    parts = jnp.concatenate(
        [jnp.where(own_first, own, other), jnp.where(own_first, other, own)], axis=0
    )
    parts = lax.all_to_all(
        parts,
        ("tm", "chan"),
        0,
        0,
        axis_index_groups=group_order(tm_count, chan_count),
        tiled=True,
    )
    power = pl.pallas_call(
        accel_search,
        out_shape=jax.ShapeDtypeStruct((accels * TRIAL_DEV, block_len // 2), jnp.bfloat16),
        scratch_shapes=[
            pltpu.VMEM((2 * block_len, TRIAL_DEV * block_len // 2), jnp.bfloat16),
            pltpu.VMEM((accels * TRIAL_DEV, block_len // 2), jnp.float32),
        ],
        compiler_params=pltpu.CompilerParams(vmem_limit_bytes=40 * 1024 * 1024),
        name="accel_search",
    )(parts, bin_table(block_len), kernels)
    return power.reshape(accels, TRIAL_DEV, block_len // 2)


def solution(mesh):
    placed = (P("chan", "tm"), P(), P(), P())
    return jax.shard_map(
        functools.partial(shards, mesh.shape["tm"], mesh.shape["chan"]),
        mesh=mesh,
        in_specs=placed,
        out_specs=P(None, "chan", "tm"),
        check_vma=False,
    )
```

```python
import functools
import math

import jax
import jax.numpy as jnp
import numpy as np
from jax import lax
from jax.experimental import pallas as pl
from jax.experimental.pallas import tpu as pltpu
from jax.sharding import PartitionSpec as P

TRIAL_DEV = 4
MAXDELAY = 4096
LANES = 128
STEP = 8
ROWS = 2 * TRIAL_DEV


def bin_table(block_len):
    half_len = block_len // 2
    samples = np.arange(half_len)
    angles = (samples[:, None] * samples[None, :] % block_len) * (2.0 * math.pi / block_len)
    table = np.concatenate([np.cos(angles), -np.sin(angles)], axis=1)
    return jnp.asarray(table.astype(np.float32), jnp.bfloat16)


def shift_left(value, steps):
    width = value.shape[1]
    return pltpu.roll(value, width - steps, 1)


def as_column(row):
    count = row.shape[1]
    rows = lax.broadcasted_iota(jnp.int32, (count, count), 0)
    columns = lax.broadcasted_iota(jnp.int32, (count, count), 1)
    return jnp.sum(jnp.where(rows == columns, row, 0.0), axis=1, keepdims=True)


def chan_order(chan_count):
    return [chan_count - 1] + list(range(chan_count - 1))


def trial_blocks(value, chan_count):
    parts = []
    for owner in chan_order(chan_count):
        rows = value[owner * TRIAL_DEV : (owner + 1) * TRIAL_DEV]
        parts += [rows[:, :LANES], rows[:, LANES:]]
    return jnp.concatenate(parts, axis=0)


def group_order(tm_count, chan_count):
    groups = []
    for odd in range(1, tm_count, 2):
        blocks = sorted((odd, (odd + 1) % tm_count))
        groups.append(
            [block * chan_count + owner for block in blocks for owner in chan_order(chan_count)]
        )
    return groups


def fold(total, trials, block_len):
    width = total.shape[1]
    repeats = width // trials
    repeat_of = lax.broadcasted_iota(jnp.int32, (block_len, width), 1) // trials
    sums = total[:block_len]
    for repeat in range(1, repeats):
        first = repeat * STEP
        sums = jnp.where(repeat_of == repeat, total[first : first + block_len], sums)
    turned_back = sums.T
    return sum(turned_back[repeat * trials : (repeat + 1) * trials] for repeat in range(repeats))


def partial_series(
    chan_count,
    samples_hbm,
    delay_hbm,
    tail_hbm,
    table_hbm,
    kernels_hbm,
    early_ref,
    moved,
    chosen,
    top_bin_ref,
    table_ref,
    kernels_ref,
    samples_ref,
    delay_ref,
    tail_ref,
    turned,
    total,
    arrived,
):
    channels, block_len = samples_ref.shape
    trials = tail_ref.shape[1]
    repeats = max(1, LANES // trials)
    width = repeats * trials
    groups = block_len // (STEP * repeats)
    pair = max(1, 2 * LANES // width)
    copies = [
        pltpu.make_async_copy(source, target, arrived.at[index])
        for index, (source, target) in enumerate(
            [(delay_hbm, delay_ref), (tail_hbm, tail_ref), (samples_hbm, samples_ref)]
        )
    ]
    for copy in copies:
        copy.start()
    copies[0].wait()
    copies[1].wait()

    delays = as_column(delay_ref[pl.ds(lax.axis_index("chan"), 1), :].astype(jnp.float32))
    tails = jnp.concatenate([tail_ref[...].astype(jnp.float32)] * repeats, axis=1)
    shifts = jnp.floor(delays * tails * (1.0 / MAXDELAY))
    columns = lax.broadcasted_iota(jnp.int32, (channels, width), 1)
    repeat_of = columns // trials
    rests = (shifts - STEP * repeat_of.astype(jnp.float32)).astype(jnp.bfloat16)
    one = jnp.ones((), jnp.bfloat16)
    zero = jnp.zeros((), jnp.bfloat16)

    def where_rest_is(value):
        return jnp.where(rests == jnp.array(value, jnp.bfloat16), one, zero)

    def choose(first):
        for fine in range(STEP):
            for group in range(first, min(first + pair, groups)):
                chosen[
                    fine * channels : (fine + 1) * channels, group * width : (group + 1) * width
                ] = where_rest_is(STEP * repeats * group + fine)

    firsts = list(range(0, groups, pair))
    half = len(firsts) // 2
    firsts = firsts[half:][::-1] + firsts[:half]
    for first in firsts[:1]:
        choose(first)
    own_shifts = shifts[:, :trials]
    whole = jnp.where(own_shifts == block_len, one, zero)
    parity = jnp.where(own_shifts - 2.0 * jnp.floor(own_shifts * 0.5) == 0.0, one, -one)

    copies[2].wait()
    copies = [
        pltpu.make_async_copy(table_hbm, table_ref, arrived.at[3]),
        pltpu.make_async_copy(kernels_hbm, kernels_ref, arrived.at[4]),
    ]
    for copy in copies:
        copy.start()
    rows = moved.shape[0]
    turned[:STEP] = jnp.zeros((STEP, channels), jnp.float32)
    turned[STEP : STEP + block_len] = samples_ref[...].T.astype(jnp.float32)
    turned[STEP + block_len :] = jnp.zeros((2 * STEP, channels), jnp.float32)
    for fine in range(STEP):
        moved[:, fine * channels : (fine + 1) * channels] = turned[fine : fine + rows].astype(
            jnp.bfloat16
        )
    step = STEP * repeats
    end = block_len + step - STEP
    total[...] = jnp.zeros_like(total)
    for index, first in enumerate(firsts):
        if index >= 1:
            choose(first)
        last = min(first + pair, groups)
        sums = jnp.dot(
            moved[: step * last],
            chosen[:, first * width : last * width],
            preferred_element_type=jnp.float32,
        )
        for group in range(first, last):
            columns_of = slice((group - first) * width, (group - first + 1) * width)
            total[end - step * (group + 1) : end] += sums[: step * (group + 1), columns_of]
    signs = lax.broadcasted_iota(jnp.int32, (block_len, block_len), 0)
    signs += lax.broadcasted_iota(jnp.int32, (block_len, block_len), 1)
    nyquist_step = 0.5 / block_len
    alternating = jnp.where(signs % 2 == 0, -nyquist_step, nyquist_step).astype(jnp.bfloat16)
    samples = samples_ref[...]
    nyquist = jnp.dot(samples, alternating, preferred_element_type=jnp.float32)
    over_channels = (((0,), (0,)), ((), ()))
    top_bin = lax.dot_general(
        parity, nyquist.astype(jnp.bfloat16), over_channels, preferred_element_type=jnp.float32
    )
    whole_block = lax.dot_general(
        whole, samples, over_channels, preferred_element_type=jnp.float32
    )
    early = fold(total, trials, block_len) + top_bin + whole_block
    positions = lax.broadcasted_iota(jnp.int32, (trials, block_len), 1)
    kept = positions.astype(jnp.float32) >= block_len - as_column(tails[:, :trials])
    early = jnp.where(kept, early, 0.0) * (1.0 / math.sqrt(channels * chan_count))
    early_ref[...] = trial_blocks(early, chan_count).astype(jnp.bfloat16)
    top_bin_ref[...] = top_bin
    for copy in copies:
        copy.wait()


def late_series(chan_count, scale, moved, chosen, top_bin_ref, late_ref, total):
    trials, block_len = top_bin_ref.shape
    repeats = max(1, LANES // trials)
    width = repeats * trials
    step = STEP * repeats
    groups = block_len // step
    pair = max(1, 2 * LANES // width)
    total[...] = jnp.zeros_like(total)
    for first in range(0, groups, pair):
        last = min(first + pair, groups)
        start = step * first
        sums = jnp.dot(
            moved[start:], chosen[:, first * width : last * width], preferred_element_type=jnp.float32
        )
        for group in range(first, last):
            columns_of = slice((group - first) * width, (group - first + 1) * width)
            rows_of = slice(step * group + STEP - start, block_len + STEP - start)
            total[: block_len - step * group] += sums[rows_of, columns_of]
    late = (fold(total, trials, block_len) + top_bin_ref[...]) * scale
    late_ref[...] = trial_blocks(late, chan_count)


def accel_search(
    parts_ref, table_ref, kernels_ref, out_ref, windows, by_kernel
):
    sources = parts_ref.shape[0] // ROWS
    parts = parts_ref[...].astype(jnp.float32).reshape(sources, ROWS, LANES)
    series = jnp.sum(parts, axis=0).astype(jnp.bfloat16)

    half_len = LANES
    block_len = 2 * half_len
    halves = jnp.dot(series, table_ref[...], preferred_element_type=jnp.float32)
    columns = lax.broadcasted_iota(jnp.int32, (TRIAL_DEV, block_len), 1)
    signs = jnp.where(columns % 2 == 0, 1.0, -1.0)
    spectra = (halves[:TRIAL_DEV] + signs * halves[TRIAL_DEV:]) * (1.0 / math.sqrt(block_len))
    spectra = spectra.astype(jnp.bfloat16).astype(jnp.float32)

    taps = lax.broadcasted_iota(jnp.int32, (half_len, half_len), 0)
    bins = lax.broadcasted_iota(jnp.int32, (half_len, half_len), 1)
    early = bins <= taps
    zero = jnp.zeros((), jnp.bfloat16)
    for trial in range(TRIAL_DEV):
        for part in range(2):
            row = spectra[trial : trial + 1, part * half_len : (part + 1) * half_len]
            turned = pltpu.roll(
                jnp.broadcast_to(row, (half_len, half_len)), 1, 1, stride=1, stride_axis=0
            ).astype(jnp.bfloat16)
            first = part * block_len
            columns_of = slice(trial * half_len, (trial + 1) * half_len)
            windows[first : first + half_len, columns_of] = jnp.where(early, turned, zero)
            windows[first + half_len : first + block_len, columns_of] = jnp.where(
                early, zero, turned
            )

    ends = lax.broadcasted_iota(jnp.int32, (block_len, block_len), 0)
    ends += lax.broadcasted_iota(jnp.int32, (block_len, block_len), 1)
    reverse = jnp.where(ends == block_len - 1, 1.0, 0.0).astype(jnp.bfloat16)
    real, imag = (
        jnp.dot(kernels_ref[part], reverse, preferred_element_type=jnp.float32).astype(
            jnp.bfloat16
        )
        for part in range(2)
    )
    weights = jnp.concatenate(
        [jnp.concatenate([real, -imag], axis=1), jnp.concatenate([imag, real], axis=1)], axis=0
    )
    correlation = jnp.dot(weights, windows[...], preferred_element_type=jnp.float32)
    accels = real.shape[0]
    power = correlation[:accels] * correlation[:accels] + correlation[accels:] * correlation[accels:]
    for trial in range(TRIAL_DEV):
        by_kernel[pl.ds(trial, accels, stride=TRIAL_DEV), :] = power[
            :, trial * half_len : (trial + 1) * half_len
        ]
    out_ref[...] = by_kernel[...].astype(jnp.bfloat16)


def shards(tm_count, chan_count, filterbank, chan_delay, tail_len, kernels):
    channels, block_len = filterbank.shape
    trials = tail_len.shape[0]
    accels = kernels.shape[1]
    total_rows = block_len + STEP * (max(1, LANES // trials) - 1)
    total = pltpu.VMEM((total_rows, max(LANES, trials)), jnp.float32)
    group_rows = chan_count * ROWS
    table = bin_table(block_len)
    early, moved, chosen, top_bin, table_copy, kernels_copy = pl.pallas_call(
        functools.partial(partial_series, chan_count),
        out_shape=(
            jax.ShapeDtypeStruct((group_rows, LANES), jnp.bfloat16),
            jax.ShapeDtypeStruct((block_len + 2 * STEP, STEP * channels), jnp.bfloat16),
            jax.ShapeDtypeStruct((STEP * channels, block_len // STEP * trials), jnp.bfloat16),
            jax.ShapeDtypeStruct((trials, block_len), jnp.float32),
            jax.ShapeDtypeStruct(table.shape, table.dtype),
            jax.ShapeDtypeStruct(kernels.shape, kernels.dtype),
        ),
        in_specs=[pl.BlockSpec(memory_space=pltpu.HBM)] * 5,
        scratch_shapes=[
            pltpu.VMEM((channels, block_len), jnp.bfloat16),
            pltpu.VMEM((chan_count, channels), jnp.int32),
            pltpu.VMEM((1, trials), jnp.int32),
            pltpu.VMEM((block_len + 3 * STEP, channels), jnp.float32),
            total,
            pltpu.SemaphoreType.DMA((5,)),
        ],
        compiler_params=pltpu.CompilerParams(vmem_limit_bytes=40 * 1024 * 1024),
        name="partial_series",
    )(
        *(
            pltpu.with_memory_space_constraint(value, pltpu.HBM)
            for value in (
                filterbank,
                chan_delay.reshape(chan_count, channels),
                tail_len.reshape(1, trials),
                table,
                kernels,
            )
        )
    )
    tails = lax.ppermute(early, "tm", [(index, index ^ 1) for index in range(tm_count)])
    late = pl.pallas_call(
        functools.partial(late_series, chan_count, 1.0 / math.sqrt(channels * chan_count)),
        out_shape=jax.ShapeDtypeStruct((group_rows, LANES), jnp.float32),
        scratch_shapes=[total],
        compiler_params=pltpu.CompilerParams(vmem_limit_bytes=16 * 1024 * 1024),
        cost_estimate=pl.CostEstimate(
            flops=2 * block_len * STEP * channels * block_len // STEP * trials,
            bytes_accessed=4 * block_len * block_len,
            transcendentals=0,
        ),
        name="late_series",
    )(moved, chosen, top_bin)
    block = lax.axis_index("tm")
    is_even = block % 2 == 0
    own = (late + jnp.where(is_even, tails.astype(jnp.float32), 0.0)).astype(jnp.bfloat16)
    other = jnp.where(jnp.logical_and(is_even, block > 0), early, jnp.zeros_like(early))
    own_first = jnp.where(is_even, block == 0, block < tm_count - 1)
    parts = jnp.concatenate(
        [jnp.where(own_first, own, other), jnp.where(own_first, other, own)], axis=0
    )
    parts = lax.all_to_all(
        parts,
        ("tm", "chan"),
        0,
        0,
        axis_index_groups=group_order(tm_count, chan_count),
        tiled=True,
    )
    power = pl.pallas_call(
        accel_search,
        out_shape=jax.ShapeDtypeStruct((accels * TRIAL_DEV, block_len // 2), jnp.bfloat16),
        scratch_shapes=[
            pltpu.VMEM((2 * block_len, TRIAL_DEV * block_len // 2), jnp.bfloat16),
            pltpu.VMEM((accels * TRIAL_DEV, block_len // 2), jnp.float32),
        ],
        compiler_params=pltpu.CompilerParams(vmem_limit_bytes=40 * 1024 * 1024),
        name="accel_search",
    )(parts, table_copy, kernels_copy)
    return power.reshape(accels, TRIAL_DEV, block_len // 2)


def solution(mesh):
    placed = (P("chan", "tm"), P(), P(), P())
    return jax.shard_map(
        functools.partial(shards, mesh.shape["tm"], mesh.shape["chan"]),
        mesh=mesh,
        in_specs=placed,
        out_specs=P(None, "chan", "tm"),
        check_vma=False,
    )
```

```python
import functools
import math

import jax
import jax.numpy as jnp
import numpy as np
from jax import lax
from jax.experimental import pallas as pl
from jax.experimental.pallas import tpu as pltpu
from jax.sharding import PartitionSpec as P

TRIAL_DEV = 4
MAXDELAY = 4096
LANES = 128
STEP = 8
ROWS = 2 * TRIAL_DEV


def bin_table(block_len):
    half_len = block_len // 2
    samples = np.arange(half_len)
    angles = (samples[:, None] * samples[None, :] % block_len) * (2.0 * math.pi / block_len)
    table = np.concatenate([np.cos(angles), -np.sin(angles)], axis=1)
    return jnp.asarray(table.astype(np.float32), jnp.bfloat16)


def shift_left(value, steps):
    width = value.shape[1]
    return pltpu.roll(value, width - steps, 1)


def as_column(row):
    count = row.shape[1]
    rows = lax.broadcasted_iota(jnp.int32, (count, count), 0)
    columns = lax.broadcasted_iota(jnp.int32, (count, count), 1)
    return jnp.sum(jnp.where(rows == columns, row, 0.0), axis=1, keepdims=True)


def chan_order(chan_count):
    return [chan_count - 1] + list(range(chan_count - 1))


def trial_blocks(value, chan_count):
    parts = []
    for owner in chan_order(chan_count):
        rows = value[owner * TRIAL_DEV : (owner + 1) * TRIAL_DEV]
        parts += [rows[:, :LANES], rows[:, LANES:]]
    return jnp.concatenate(parts, axis=0)


def group_order(tm_count, chan_count):
    groups = []
    for odd in range(1, tm_count, 2):
        blocks = sorted((odd, (odd + 1) % tm_count))
        groups.append(
            [block * chan_count + owner for block in blocks for owner in chan_order(chan_count)]
        )
    return groups


def fold(total, trials, block_len):
    width = total.shape[1]
    repeats = width // trials
    repeat_of = lax.broadcasted_iota(jnp.int32, (block_len, width), 1) // trials
    sums = total[:block_len]
    for repeat in range(1, repeats):
        first = repeat * STEP
        sums = jnp.where(repeat_of == repeat, total[first : first + block_len], sums)
    turned_back = sums.T
    return sum(turned_back[repeat * trials : (repeat + 1) * trials] for repeat in range(repeats))


def partial_series(
    chan_count,
    samples_hbm,
    delay_hbm,
    tail_hbm,
    early_ref,
    moved,
    chosen,
    top_bin_ref,
    samples_ref,
    delay_ref,
    tail_ref,
    turned,
    total,
    arrived,
):
    channels, block_len = samples_ref.shape
    trials = tail_ref.shape[1]
    repeats = max(1, LANES // trials)
    width = repeats * trials
    groups = block_len // (STEP * repeats)
    pair = max(1, 2 * LANES // width)
    copies = [
        pltpu.make_async_copy(source, target, arrived.at[index])
        for index, (source, target) in enumerate(
            [(delay_hbm, delay_ref), (tail_hbm, tail_ref), (samples_hbm, samples_ref)]
        )
    ]
    for copy in copies:
        copy.start()
    copies[0].wait()
    copies[1].wait()

    delays = as_column(delay_ref[pl.ds(lax.axis_index("chan"), 1), :].astype(jnp.float32))
    tails = jnp.concatenate([tail_ref[...].astype(jnp.float32)] * repeats, axis=1)
    shifts = jnp.floor(delays * tails * (1.0 / MAXDELAY))
    columns = lax.broadcasted_iota(jnp.int32, (channels, width), 1)
    repeat_of = columns // trials
    rests = (shifts - STEP * repeat_of.astype(jnp.float32)).astype(jnp.bfloat16)
    one = jnp.ones((), jnp.bfloat16)
    zero = jnp.zeros((), jnp.bfloat16)

    def where_rest_is(value):
        return jnp.where(rests == jnp.array(value, jnp.bfloat16), one, zero)

    def choose(first, fines=range(STEP)):
        for fine in fines:
            for group in range(first, min(first + pair, groups)):
                chosen[
                    fine * channels : (fine + 1) * channels, group * width : (group + 1) * width
                ] = where_rest_is(STEP * repeats * group + fine)

    firsts = list(range(0, groups, pair))
    half = len(firsts) // 2
    firsts = firsts[half:][::-1] + firsts[:half]
    choose(firsts[0], range(STEP // 2))
    own_shifts = shifts[:, :trials]
    whole = jnp.where(own_shifts == block_len, one, zero)
    parity = jnp.where(own_shifts - 2.0 * jnp.floor(own_shifts * 0.5) == 0.0, one, -one)

    copies[2].wait()
    rows = moved.shape[0]
    turned[:STEP] = jnp.zeros((STEP, channels), jnp.float32)
    turned[STEP : STEP + block_len] = samples_ref[...].T.astype(jnp.float32)
    turned[STEP + block_len :] = jnp.zeros((2 * STEP, channels), jnp.float32)
    for fine in range(STEP):
        moved[:, fine * channels : (fine + 1) * channels] = turned[fine : fine + rows].astype(
            jnp.bfloat16
        )
    step = STEP * repeats
    end = block_len + step - STEP
    total[...] = jnp.zeros_like(total)
    for index, first in enumerate(firsts):
        if index == 0:
            choose(first, range(STEP // 2, STEP))
        else:
            choose(first)
        last = min(first + pair, groups)
        sums = jnp.dot(
            moved[: step * last],
            chosen[:, first * width : last * width],
            preferred_element_type=jnp.float32,
        )
        for group in range(first, last):
            columns_of = slice((group - first) * width, (group - first + 1) * width)
            total[end - step * (group + 1) : end] += sums[: step * (group + 1), columns_of]
    signs = lax.broadcasted_iota(jnp.int32, (block_len, block_len), 0)
    signs += lax.broadcasted_iota(jnp.int32, (block_len, block_len), 1)
    nyquist_step = 0.5 / block_len
    alternating = jnp.where(signs % 2 == 0, -nyquist_step, nyquist_step).astype(jnp.bfloat16)
    samples = samples_ref[...]
    nyquist = jnp.dot(samples, alternating, preferred_element_type=jnp.float32)
    over_channels = (((0,), (0,)), ((), ()))
    top_bin = lax.dot_general(
        parity, nyquist.astype(jnp.bfloat16), over_channels, preferred_element_type=jnp.float32
    )
    whole_block = lax.dot_general(
        whole, samples, over_channels, preferred_element_type=jnp.float32
    )
    early = fold(total, trials, block_len) + top_bin + whole_block
    positions = lax.broadcasted_iota(jnp.int32, (trials, block_len), 1)
    kept = positions.astype(jnp.float32) >= block_len - as_column(tails[:, :trials])
    early = jnp.where(kept, early, 0.0) * (1.0 / math.sqrt(channels * chan_count))
    early_ref[...] = trial_blocks(early, chan_count).astype(jnp.bfloat16)
    top_bin_ref[...] = top_bin


def late_series(chan_count, scale, moved, chosen, top_bin_ref, late_ref, total):
    trials, block_len = top_bin_ref.shape
    repeats = max(1, LANES // trials)
    width = repeats * trials
    step = STEP * repeats
    groups = block_len // step
    pair = max(1, 2 * LANES // width)
    total[...] = jnp.zeros_like(total)
    for first in range(0, groups, pair):
        last = min(first + pair, groups)
        start = step * first
        sums = jnp.dot(
            moved[start:], chosen[:, first * width : last * width], preferred_element_type=jnp.float32
        )
        for group in range(first, last):
            columns_of = slice((group - first) * width, (group - first + 1) * width)
            rows_of = slice(step * group + STEP - start, block_len + STEP - start)
            total[: block_len - step * group] += sums[rows_of, columns_of]
    late = (fold(total, trials, block_len) + top_bin_ref[...]) * scale
    late_ref[...] = trial_blocks(late, chan_count)


def accel_search(
    parts_ref, table_ref, kernels_ref, out_ref, windows, by_kernel
):
    sources = parts_ref.shape[0] // ROWS
    parts = parts_ref[...].astype(jnp.float32).reshape(sources, ROWS, LANES)
    series = jnp.sum(parts, axis=0).astype(jnp.bfloat16)

    half_len = LANES
    block_len = 2 * half_len
    halves = jnp.dot(series, table_ref[...], preferred_element_type=jnp.float32)
    columns = lax.broadcasted_iota(jnp.int32, (TRIAL_DEV, block_len), 1)
    signs = jnp.where(columns % 2 == 0, 1.0, -1.0)
    spectra = (halves[:TRIAL_DEV] + signs * halves[TRIAL_DEV:]) * (1.0 / math.sqrt(block_len))
    spectra = spectra.astype(jnp.bfloat16).astype(jnp.float32)

    taps = lax.broadcasted_iota(jnp.int32, (half_len, half_len), 0)
    bins = lax.broadcasted_iota(jnp.int32, (half_len, half_len), 1)
    early = bins <= taps
    zero = jnp.zeros((), jnp.bfloat16)
    for trial in range(TRIAL_DEV):
        for part in range(2):
            row = spectra[trial : trial + 1, part * half_len : (part + 1) * half_len]
            turned = pltpu.roll(
                jnp.broadcast_to(row, (half_len, half_len)), 1, 1, stride=1, stride_axis=0
            ).astype(jnp.bfloat16)
            first = part * block_len
            columns_of = slice(trial * half_len, (trial + 1) * half_len)
            windows[first : first + half_len, columns_of] = jnp.where(early, turned, zero)
            windows[first + half_len : first + block_len, columns_of] = jnp.where(
                early, zero, turned
            )

    ends = lax.broadcasted_iota(jnp.int32, (block_len, block_len), 0)
    ends += lax.broadcasted_iota(jnp.int32, (block_len, block_len), 1)
    reverse = jnp.where(ends == block_len - 1, 1.0, 0.0).astype(jnp.bfloat16)
    real, imag = (
        jnp.dot(kernels_ref[part], reverse, preferred_element_type=jnp.float32).astype(
            jnp.bfloat16
        )
        for part in range(2)
    )
    weights = jnp.concatenate(
        [jnp.concatenate([real, -imag], axis=1), jnp.concatenate([imag, real], axis=1)], axis=0
    )
    correlation = jnp.dot(weights, windows[...], preferred_element_type=jnp.float32)
    accels = real.shape[0]
    power = correlation[:accels] * correlation[:accels] + correlation[accels:] * correlation[accels:]
    for trial in range(TRIAL_DEV):
        by_kernel[pl.ds(trial, accels, stride=TRIAL_DEV), :] = power[
            :, trial * half_len : (trial + 1) * half_len
        ]
    out_ref[...] = by_kernel[...].astype(jnp.bfloat16)


def shards(tm_count, chan_count, filterbank, chan_delay, tail_len, kernels):
    channels, block_len = filterbank.shape
    trials = tail_len.shape[0]
    accels = kernels.shape[1]
    total_rows = block_len + STEP * (max(1, LANES // trials) - 1)
    total = pltpu.VMEM((total_rows, max(LANES, trials)), jnp.float32)
    group_rows = chan_count * ROWS
    early, moved, chosen, top_bin = pl.pallas_call(
        functools.partial(partial_series, chan_count),
        out_shape=(
            jax.ShapeDtypeStruct((group_rows, LANES), jnp.bfloat16),
            jax.ShapeDtypeStruct((block_len + 2 * STEP, STEP * channels), jnp.bfloat16),
            jax.ShapeDtypeStruct((STEP * channels, block_len // STEP * trials), jnp.bfloat16),
            jax.ShapeDtypeStruct((trials, block_len), jnp.float32),
        ),
        in_specs=[pl.BlockSpec(memory_space=pltpu.HBM)] * 3,
        scratch_shapes=[
            pltpu.VMEM((channels, block_len), jnp.bfloat16),
            pltpu.VMEM((chan_count, channels), jnp.int32),
            pltpu.VMEM((1, trials), jnp.int32),
            pltpu.VMEM((block_len + 3 * STEP, channels), jnp.float32),
            total,
            pltpu.SemaphoreType.DMA((3,)),
        ],
        compiler_params=pltpu.CompilerParams(vmem_limit_bytes=40 * 1024 * 1024),
        name="partial_series",
    )(
        *(
            pltpu.with_memory_space_constraint(value, pltpu.HBM)
            for value in (
                filterbank,
                chan_delay.reshape(chan_count, channels),
                tail_len.reshape(1, trials),
            )
        )
    )
    tails = lax.ppermute(early, "tm", [(index, index ^ 1) for index in range(tm_count)])
    late = pl.pallas_call(
        functools.partial(late_series, chan_count, 1.0 / math.sqrt(channels * chan_count)),
        out_shape=jax.ShapeDtypeStruct((group_rows, LANES), jnp.float32),
        scratch_shapes=[total],
        compiler_params=pltpu.CompilerParams(vmem_limit_bytes=16 * 1024 * 1024),
        cost_estimate=pl.CostEstimate(
            flops=2 * block_len * STEP * channels * block_len // STEP * trials,
            bytes_accessed=4 * block_len * block_len,
            transcendentals=0,
        ),
        name="late_series",
    )(moved, chosen, top_bin)
    block = lax.axis_index("tm")
    is_even = block % 2 == 0
    own = (late + jnp.where(is_even, tails.astype(jnp.float32), 0.0)).astype(jnp.bfloat16)
    other = jnp.where(jnp.logical_and(is_even, block > 0), early, jnp.zeros_like(early))
    own_first = jnp.where(is_even, block == 0, block < tm_count - 1)
    parts = jnp.concatenate(
        [jnp.where(own_first, own, other), jnp.where(own_first, other, own)], axis=0
    )
    parts = lax.all_to_all(
        parts,
        ("tm", "chan"),
        0,
        0,
        axis_index_groups=group_order(tm_count, chan_count),
        tiled=True,
    )
    power = pl.pallas_call(
        accel_search,
        out_shape=jax.ShapeDtypeStruct((accels * TRIAL_DEV, block_len // 2), jnp.bfloat16),
        scratch_shapes=[
            pltpu.VMEM((2 * block_len, TRIAL_DEV * block_len // 2), jnp.bfloat16),
            pltpu.VMEM((accels * TRIAL_DEV, block_len // 2), jnp.float32),
        ],
        compiler_params=pltpu.CompilerParams(vmem_limit_bytes=40 * 1024 * 1024),
        name="accel_search",
    )(parts, bin_table(block_len), kernels)
    return power.reshape(accels, TRIAL_DEV, block_len // 2)


def solution(mesh):
    placed = (P("chan", "tm"), P(), P(), P())
    return jax.shard_map(
        functools.partial(shards, mesh.shape["tm"], mesh.shape["chan"]),
        mesh=mesh,
        in_specs=placed,
        out_specs=P(None, "chan", "tm"),
        check_vma=False,
    )
```
